32 devices in a mesh: design: 2 (over y), gx: 4 (over z), gy: 2 (over x), src: 2 (over core).
Axes of the slice: x: 2, y: 2, z: 4, core: 2. Of those that a mesh axis runs over, the one named last changes fastest.
Arguments:
- field_state: float32 [4, 2, 2, 6, 32, 8, 512], P(('design', 'src'), None, None, None, None, 'gx', 'gy'), parts along dimension 0, may hold values from -6 to 6
- material_map: int32 [64, 8, 512], P('design', 'gx', 'gy'), parts along dimension 0, may hold values from 0 to 7
- eps_table: float32 [8], replicated, may hold values from 1 to 12
- bloch_phase: float32 [4], P('design'), parts along dimension 0, may hold values from -3.140625 to 3.140625
- source_cells: int32 [4, 2], P(('design', 'src')), parts along dimension 0, may hold values from 0 to 131071
- source_wave: float32 [4, 2, 2, 2], P(('design', 'src')), parts along dimension 0, may hold values from -8 to 8
Outputs:
- gradient: float32 [64, 8, 512], P('design', 'gx', 'gy'), parts along dimension 0
The draws below stay inside these ranges and needn't reach their ends.
There are 2 independent parts, one for each index of `design`. The reference program is written for one: setup_inputs(seed, part) draws one part's arguments, and reference() takes and returns one part's arrays. A program takes and returns all parts, laid end to end along the dimension named above; an argument that names none is the same for every part. Nothing has to cross between parts.
All inputs are finite; a program needn't handle non-finite values.
Results may differ from the reference program's by a relative error of at most 0.0001.
Values sent between devices are 32-bit elements; how exact they have to be, the bound alone decides.
No kernel may reach another device: no remote copies, remote signals or barrier semaphores. Data moves between devices by JAX's collectives and lax.ppermute only.
A program may use at most 64 MiB of HBM per device.

```python
import math
import jax
import jax.numpy as jnp
from jax import lax

NZ = 32
STEPS = 2
NMAT = 8
NSRC = 2
NX = 8
NY = 512


def with_ends(entries, own_key, low, high):
    longest = entries.shape.index(max(entries.shape))
    spots = []
    for shift in (0, 1):
        where = [jax.random.randint(jax.random.fold_in(own_key, axis), (), 0, length) for axis, length in enumerate(entries.shape)]
        where[longest] = (where[longest] + shift) % entries.shape[longest]
        spots.append(tuple(where))
    return entries.at[spots[0]].set(low).at[spots[1]].set(high)


def level_of(rng, extent, shards, least, largest):
    loudness = 1.0
    for axis_at, shards_of in shards:
        draws = jax.random.uniform(jax.random.fold_in(jax.random.fold_in(rng, 6), axis_at), (shards_of,), jnp.float32, least / len(shards), largest / len(shards))
        loudness = loudness * jnp.repeat(jnp.exp(draws), extent[axis_at] // shards_of).reshape((-1,) + (1,) * (len(extent) - 1 - axis_at))
    return loudness


def noise(key, shape, spread, limit, pieces=(), kind=jnp.bfloat16):
    result = jax.random.normal(key, shape, jnp.float32) * spread
    if len(pieces) > 0:
        result = level_of(key, shape, pieces, -0.22, 0.18) * result
    return jnp.clip(result, min=-limit, max=limit).astype(kind)


def setup_inputs(seed: int = 0, part: int = 0) -> dict:
    key_list = jax.random.split(jax.random.key(seed), 7)
    part_keys = jax.random.split(jax.random.fold_in(key_list[6], part), 7)
    return {
        "field_state": noise(part_keys[0], (NSRC, 2, 2, 6, NZ, NX, NY), 1.0, 6.0, ((0, 2), (5, 4), (6, 2)), jnp.float32),
        "material_map": with_ends(jax.random.randint(part_keys[1], (NZ, NX, NY), 0, NMAT), jax.random.fold_in(part_keys[1], 1), 0, NMAT - 1).astype(jnp.int32),
        "eps_table": jnp.clip(jnp.exp(jax.random.uniform(key_list[2], (NMAT,), jnp.float32, math.log(1.0), math.log(12.0))), 1.0, 12.0),
        "bloch_phase": jnp.clip(jax.random.uniform(part_keys[3], (2,), jnp.float32, -3.140625, 3.140625), -3.140625, 3.140625),
        "source_cells": with_ends(jax.random.randint(part_keys[4], (NSRC, 2), 0, NZ * NX * NY), jax.random.fold_in(part_keys[4], 1), 0, (NZ * NX * NY) - 1).astype(jnp.int32),
        "source_wave": noise(part_keys[5], (NSRC, 2, 2, STEPS), 2.0, 8.0, ((0, 2),), jnp.float32),
    }


COURANT = 0.5


def rotate(values, cosine, sine_part):
    real_part = values[:, 0]
    imag_part = values[:, 1]
    return jnp.stack([real_part * cosine - imag_part * sine_part, real_part * sine_part + imag_part * cosine], axis=1)


def above_z(values):
    return jnp.concatenate([values[:, :, :, 1:], jnp.zeros_like(values[:, :, :, :1])], axis=3)


def below_z(values):
    return jnp.concatenate([jnp.zeros_like(values[:, :, :, :1]), values[:, :, :, :-1]], axis=3)


def advance_h(field_e, field_h, ahead_x, ahead_y):
    upper_e = above_z(field_e[:, :, 0:2])
    curl_x = (ahead_y[:, :, 1] - field_e[:, :, 2]) - (upper_e[:, :, 1] - field_e[:, :, 1])
    curl_y = (upper_e[:, :, 0] - field_e[:, :, 0]) - (ahead_x[:, :, 1] - field_e[:, :, 2])
    curl_z = (ahead_x[:, :, 0] - field_e[:, :, 1]) - (ahead_y[:, :, 0] - field_e[:, :, 0])
    return field_h - COURANT * jnp.stack([curl_x, curl_y, curl_z], axis=2)


def advance_e(field_e, field_h, behind_x, behind_y, eps_inv, source):
    lower_h = below_z(field_h[:, :, 0:2])
    curl_x = (field_h[:, :, 2] - behind_y[:, :, 1]) - (field_h[:, :, 1] - lower_h[:, :, 1])
    curl_y = (field_h[:, :, 0] - lower_h[:, :, 0]) - (field_h[:, :, 2] - behind_x[:, :, 1])
    curl_z = (field_h[:, :, 1] - behind_x[:, :, 0]) - (field_h[:, :, 0] - behind_y[:, :, 0])
    new_x = field_e[:, :, 0] + COURANT * eps_inv * curl_x
    new_y = field_e[:, :, 1] + COURANT * eps_inv * curl_y
    new_z = field_e[:, :, 2] + COURANT * eps_inv * curl_z + source
    return jnp.stack([new_x, new_y, new_z], axis=2)


def wrap_upper(values, along_dim, cosine, sine_part):
    length = values.shape[along_dim]
    front_row = lax.slice_in_dim(values, 0, 1, axis=along_dim)
    remainder = lax.slice_in_dim(values, 1, length, axis=along_dim)
    return jnp.concatenate([remainder, rotate(front_row, cosine, sine_part)], axis=along_dim)


def wrap_lower(values, along_dim, cosine, sine_part):
    length = values.shape[along_dim]
    back_row = lax.slice_in_dim(values, length - 1, length, axis=along_dim)
    remainder = lax.slice_in_dim(values, 0, length - 1, axis=along_dim)
    return jnp.concatenate([rotate(back_row, cosine, -sine_part), remainder], axis=along_dim)


def intersection(first_e, second_e):
    return jnp.sum(first_e[0] * second_e[0] - first_e[1] * second_e[1], axis=0)


def run_source(fields, eps_inv, source_mask, wave, phases):
    cosine_x, sine_x, cosine_y, sine_y = phases
    field_e = fields[:, :, 0:3]
    field_h = fields[:, :, 3:6]
    stored = []
    for period in range(STEPS):
        ahead_x = wrap_upper(field_e[:, :, 1:3], 4, cosine_x, sine_x)
        ahead_y = wrap_upper(field_e[:, :, 0:3:2], 5, cosine_y, sine_y)
        field_h = advance_h(field_e, field_h, ahead_x, ahead_y)
        behind_x = wrap_lower(field_h[:, :, 1:3], 4, cosine_x, sine_x)
        behind_y = wrap_lower(field_h[:, :, 0:3:2], 5, cosine_y, sine_y)
        source = source_mask[:, None] * wave[:, :, period][:, :, None, None, None]
        field_e = advance_e(field_e, field_h, behind_x, behind_y, eps_inv, source)
        stored.append(field_e)
    summed_terms = jnp.zeros(eps_inv.shape, jnp.float32)
    for period in range(STEPS):
        summed_terms = summed_terms + intersection(stored[period][0], stored[STEPS - 1 - period][1])
    return summed_terms


def reference(field_state, material_map, eps_table, bloch_phase, source_cells, source_wave):
    eps_inv = 1.0 / eps_table[material_map]
    run_sign = jnp.array([1.0, -1.0], jnp.float32)
    angle_x = run_sign * bloch_phase[0]
    angle_y = run_sign * bloch_phase[1]
    phases = (jnp.cos(angle_x).reshape(2, 1, 1, 1, 1), jnp.sin(angle_x).reshape(2, 1, 1, 1, 1),
              jnp.cos(angle_y).reshape(2, 1, 1, 1, 1), jnp.sin(angle_y).reshape(2, 1, 1, 1, 1))
    index_z = lax.broadcasted_iota(jnp.int32, (NZ, NX, NY), 0)
    index_x = lax.broadcasted_iota(jnp.int32, (NZ, NX, NY), 1)
    index_y = lax.broadcasted_iota(jnp.int32, (NZ, NX, NY), 2)
    flat_index = (index_z * NX + index_x) * NY + index_y
    summed_terms = jnp.zeros((NZ, NX, NY), jnp.float32)
    for source_id in range(NSRC):
        source_mask = (flat_index[None] == source_cells[source_id][:, None, None, None]).astype(jnp.float32)
        summed_terms = summed_terms + run_source(field_state[source_id], eps_inv, source_mask, source_wave[source_id], phases)
    return -COURANT * eps_inv * summed_terms
```

```python
import functools

import jax
import jax.numpy as jnp
from jax import lax
from jax.experimental import pallas as pl
from jax.experimental.pallas import tpu as pltpu
from jax.sharding import PartitionSpec as P

COURANT = 0.5
LANES = 128
EDGE = 4
HIGHEST = 64 * 1024 * 1024


def lane_iota(nz):
    return lax.broadcasted_iota(jnp.int32, (nz, LANES), 1)


def row_iota(nz):
    return lax.broadcasted_iota(jnp.int32, (nz, LANES), 0)


def pack_edges(values, lane):
    packed = jnp.zeros_like(values[0])
    for spot, value in enumerate(values):
        moved = pltpu.roll(value, EDGE * spot + 2, 1)
        packed = jnp.where(lane // EDGE == spot, moved, packed)
    return packed


def unpack_edge(packed, spot):
    return pltpu.roll(packed, LANES - EDGE * spot - 2, 1)


class Shifts:
    def __init__(self, nz):
        self.nz = nz
        self.row = row_iota(nz)
        self.lane = lane_iota(nz)

    def z_up(self, value):
        return jnp.where(self.row == self.nz - 1, 0.0, pltpu.roll(value, self.nz - 1, 0))

    def z_down(self, value):
        return jnp.where(self.row == 0, 0.0, pltpu.roll(value, 1, 0))

    def y_up(self, tiles):
        moved = [pltpu.roll(value, LANES - 1, 1) for value in tiles]
        count = len(tiles)
        return [jnp.where(self.lane == LANES - 1, moved[(t + 1) % count], moved[t]) for t in range(count)]

    def y_down(self, tiles):
        moved = [pltpu.roll(value, 1, 1) for value in tiles]
        count = len(tiles)
        return [jnp.where(self.lane == 0, moved[(t - 1) % count], moved[t]) for t in range(count)]


def turn(real_part, imag_part, cosine, sine):
    return real_part * cosine - imag_part * sine, real_part * sine + imag_part * cosine


def phases(phase_ref):
    row = lax.broadcasted_iota(jnp.int32, (8, LANES), 0)
    angle = jnp.where(row == 0, phase_ref[0], phase_ref[1])
    cosine, sine = jnp.cos(angle), jnp.sin(angle)
    return cosine[0:1], sine[0:1], cosine[1:2], sine[1:2]


def y_turn(cosine_y, sine_y, lane):
    first = lax.axis_index("gy") == 0
    last = lax.axis_index("gy") == lax.axis_size("gy") - 1
    upper = lane < LANES // 2
    cosine = jnp.where(upper, jnp.where(last, cosine_y, 1.0), jnp.where(first, cosine_y, 1.0))
    return cosine, jnp.where(upper, jnp.where(last, sine_y, 0.0), jnp.where(first, -sine_y, 0.0))


def inverse_eps(material, table_ref):
    level = jnp.full(material.shape, table_ref[0], jnp.float32)
    for index in range(1, table_ref.shape[0]):
        level = jnp.where(material == index, table_ref[index], level)
    return 1.0 / level


def spot_of(run, part, comp):
    return (run * 2 + part) * 6 + comp


class Local:
    def __init__(self, dims, field_ref, edge_ref, table_ref, material_ref, cells_ref, wave_ref):
        self.nz, self.width_x, self.tiles = dims
        self.field_ref, self.edge_ref = field_ref, edge_ref
        self.table_ref, self.material_ref = table_ref, material_ref
        self.cells_ref, self.wave_ref = cells_ref, wave_ref
        self.shifts = Shifts(self.nz)

    def rows(self, x, t):
        return pl.ds(t * self.width_x + x, self.nz, stride=self.tiles * self.width_x)

    def own(self, run, part, comp, x, t):
        return self.field_ref[spot_of(run, part, comp), self.rows(x, t), :]

    def edge(self, x):
        return self.edge_ref[x * self.nz:(x + 1) * self.nz, :]

    def load(self, run, comp, x, turn_y):
        cosine, sine = turn_y
        packed = self.edge(x)
        parts = [[self.own(run, part, comp, x, t) for t in range(self.tiles)] for part in range(2)]
        edges = [unpack_edge(packed, spot_of(run, part, comp)) for part in range(2)]
        edges = turn(edges[0], edges[1], cosine, sine if run == 0 else -sine)
        return [parts[part] + [edges[part]] for part in range(2)]

    def eps(self, x):
        own = [inverse_eps(self.material_ref[self.rows(x, t), :], self.table_ref) for t in range(self.tiles)]
        return own + [unpack_edge(self.edge(x), 24)]

    def hits(self, run, x):
        total_x = self.width_x * lax.axis_size("gx")
        width_y = self.tiles * LANES
        total_y = width_y * lax.axis_size("gy")
        begin_y = lax.axis_index("gy") * width_y
        plane = self.shifts.row * total_x + lax.axis_index("gx") * self.width_x + x
        masks = []
        for t in range(self.tiles + 1):
            lane = self.shifts.lane
            if t < self.tiles:
                column = begin_y + t * LANES + lane
            else:
                column = begin_y + jnp.where(lane < LANES // 2, lane + width_y, lane - LANES)
                column = jnp.where(column < 0, column + total_y, column)
                column = jnp.where(column >= total_y, column - total_y, column)
            masks.append(plane * total_y + column == self.cells_ref[run])
        return masks

    def source(self, run, step, masks, turn_y):
        cosine, sine = turn_y
        amplitude = [self.wave_ref[(run * 2 + part) * 2 + step] for part in range(2)]
        turned = turn(amplitude[0], amplitude[1], cosine, sine if run == 0 else -sine)
        return [
            [jnp.where(mask, amplitude[part] if t < self.tiles else turned[part], 0.0) for t, mask in enumerate(masks)]
            for part in range(2)
        ]


def first_kernel(dims, field_ref, material_ref, table_ref, face_ref, edge_ref):
    nz, width_x, tiles = dims
    local = Local(dims, field_ref, None, table_ref, material_ref, None, None)
    lane = lane_iota(nz)
    for run in range(2):
        for part in range(2):
            for which in range(2):
                for t in range(tiles):
                    at = (((run * 2 + part) * 2 + which) * tiles + t) * nz
                    face_ref[at:at + nz, :] = local.own(run, part, 1 + which, 0, t)
    for x in range(width_x):
        values = []
        for run in range(2):
            for part in range(2):
                for comp in range(6):
                    values.append(
                        jnp.where(
                            lane < LANES // 2,
                            local.own(run, part, comp, x, 0),
                            local.own(run, part, comp, x, tiles - 1),
                        )
                    )
        material = jnp.where(
            lane < LANES // 2, material_ref[local.rows(x, 0), :], material_ref[local.rows(x, tiles - 1), :]
        )
        values.append(inverse_eps(material, table_ref))
        edge_ref[x * nz:(x + 1) * nz, :] = pack_edges(values, lane)


def merged_edges(below_ref, above_ref, edge_ref):
    if above_ref is None:
        return below_ref
    lane = lax.broadcasted_iota(jnp.int32, below_ref.shape, 1)
    edge_ref[...] = jnp.where(lane % EDGE < 2, below_ref[...], above_ref[...])
    return edge_ref


def second_kernel(
    dims, two, field_ref, material_ref, table_ref, phase_ref, cells_ref, wave_ref, below_ref, above_ref, down_ref, up_ref,
    edge_ref,
):
    nz, width_x, tiles = dims
    edges = merged_edges(below_ref, None if two else above_ref, edge_ref)
    local = Local(dims, field_ref, edges, table_ref, material_ref, cells_ref, wave_ref)
    shifts = local.shifts
    _, _, cosine_y, sine_y = phases(phase_ref)
    turn_y = y_turn(cosine_y, sine_y, shifts.lane)
    every = range(tiles + 1)
    eps = local.eps(0)
    half = [COURANT * value for value in eps]
    down_edges = [None] * 17
    up_edges = []
    for run in range(2):
        low = [local.load(run, comp, 0, turn_y) for comp in range(6)]
        nearer = [local.load(run, comp, 1, turn_y) for comp in (1, 2)]
        source = local.source(run, 0, local.hits(run, 0), turn_y)
        for part in range(2):
            ex, ey, ez, hx, hy, hz = [low[comp][part] for comp in range(6)]
            ey_x, ez_x = nearer[0][part], nearer[1][part]
            ez_y, ex_y = shifts.y_up(ez), shifts.y_up(ex)
            hx = [hx[t] - COURANT * (ez_y[t] - ez[t] - (shifts.z_up(ey[t]) - ey[t])) for t in every]
            hy = [hy[t] - COURANT * (shifts.z_up(ex[t]) - ex[t] - (ez_x[t] - ez[t])) for t in every]
            hz = [hz[t] - COURANT * (ey_x[t] - ey[t] - (ex_y[t] - ex[t])) for t in every]
            hx_y = shifts.y_down(hx)
            new_y = [ey[t] + half[t] * (hx[t] - shifts.z_down(hx[t]) - hz[t]) for t in every]
            new_z = [ez[t] + half[t] * (hy[t] - (hx[t] - hx_y[t])) + source[part][t] for t in every]
            for which, value, initial in ((0, new_y, ey), (1, new_z, ez)):
                unit = (run * 2 + part) * 2 + which
                for t in range(tiles):
                    at = (unit * tiles + t) * nz
                    down_ref[at:at + nz, :] = value[t]
                down_edges[unit] = initial[tiles]
                down_edges[8 + unit] = value[tiles]
        high = [local.load(run, comp, width_x - 1, turn_y) for comp in (0, 1, 2, 4, 5)]
        for part in range(2):
            ex, ey, ez, hy, hz = [values[part] for values in high]
            ex_y = shifts.y_up(ex)
            hy = [hy[t] - COURANT * (shifts.z_up(ex[t]) - ex[t] + ez[t]) for t in every]
            hz = [hz[t] + COURANT * (ey[t] + (ex_y[t] - ex[t])) for t in every]
            for which, value in ((0, hy), (1, hz)):
                unit = (run * 2 + part) * 2 + which
                for t in range(tiles):
                    at = (unit * tiles + t) * nz
                    up_ref[at:at + nz, :] = value[t]
                up_edges.append(value[tiles])
    for t in range(tiles):
        at = (8 * tiles + t) * nz
        down_ref[at:at + nz, :] = eps[t]
    down_edges[16] = eps[tiles]
    at = 9 * tiles * nz
    down_ref[at:at + nz, :] = pack_edges(down_edges, shifts.lane)
    at = 8 * tiles * nz
    up_ref[at:at + nz, :] = pack_edges(up_edges, shifts.lane)


def third_kernel(
    dims, two, field_ref, material_ref, table_ref, phase_ref, cells_ref, wave_ref, below_ref, above_ref,
    face_ref, down_ref, up_ref, cross_ref, share_ref, edge_ref,
):
    nz, width_x, tiles = dims
    edges = merged_edges(below_ref, None if two else above_ref, edge_ref)
    local = Local(dims, field_ref, edges, table_ref, material_ref, cells_ref, wave_ref)
    shifts = local.shifts
    cosine_x, sine_x, cosine_y, sine_y = phases(phase_ref)
    turn_y = y_turn(cosine_y, sine_y, shifts.lane)
    first = lax.axis_index("gx") == 0
    last = lax.axis_index("gx") == lax.axis_size("gx") - 1
    ahead = (jnp.where(last, cosine_x, 1.0), jnp.where(last, sine_x, 0.0))
    back = (jnp.where(first, cosine_x, 1.0), jnp.where(first, -sine_x, 0.0))
    every = range(tiles + 1)
    own = range(tiles)
    layers = range(width_x)

    def block(ref, index):
        return ref[index * nz:(index + 1) * nz, :]

    eps = [local.eps(x) for x in layers]
    half = [[COURANT * value for value in eps[x]] for x in layers]
    down_edge = block(down_ref, 9 * tiles)
    up_edge = block(up_ref, 8 * tiles)
    eps_next = [block(down_ref, 8 * tiles + t) for t in own] + [unpack_edge(down_edge, 16)]
    half_next = [COURANT * value for value in eps_next]

    def halo(ref, edge, first_spot, run, which, cosine, sine):
        units = [(run * 2 + part) * 2 + which for part in range(2)]
        values = [
            [block(ref, unit * tiles + t) for t in own] + [unpack_edge(edge, first_spot + unit)] for unit in units
        ]
        signed = sine if run == 0 else -sine
        turned = [turn(values[0][t], values[1][t], cosine, signed) for t in every]
        return [[turned[t][part] for t in every] for part in range(2)]

    kept_one, kept_two, kept_next, kept_high = {}, {}, {}, {}
    for run in range(2):
        masks = [local.hits(run, x) for x in layers]
        sources = [[local.source(run, step, masks[x], turn_y) for x in layers] for step in range(2)]
        fields = [[local.load(run, comp, x, turn_y) for x in layers] for comp in range(6)]
        ahead_y0 = halo(face_ref, down_edge, 0, run, 0, *ahead)
        ahead_z0 = halo(face_ref, down_edge, 0, run, 1, *ahead)
        ahead_y1 = halo(down_ref, down_edge, 8, run, 0, *ahead)
        ahead_z1 = halo(down_ref, down_edge, 8, run, 1, *ahead)
        back_y = halo(up_ref, up_edge, 0, run, 0, *back)
        back_z = halo(up_ref, up_edge, 0, run, 1, *back)
        for part in range(2):
            ex, ey, ez, hx, hy, hz = [[fields[comp][x][part] for x in layers] for comp in range(6)]
            below_y = [back_y[part][t] + COURANT * ez[0][t] for t in every]
            below_z = [back_z[part][t] - COURANT * ey[0][t] for t in every]
            next_y, next_z = ahead_y0[part], ahead_z0[part]
            for step in range(2):
                ey_x, ez_x = ey[1:] + [next_y], ez[1:] + [next_z]
                for x in layers:
                    ez_y, ex_y = shifts.y_up(ez[x]), shifts.y_up(ex[x])
                    hx[x] = [hx[x][t] - COURANT * (ez_y[t] - ez[x][t] - (shifts.z_up(ey[x][t]) - ey[x][t])) for t in every]
                    hy[x] = [hy[x][t] - COURANT * (shifts.z_up(ex[x][t]) - ex[x][t] - (ez_x[x][t] - ez[x][t])) for t in every]
                    hz[x] = [hz[x][t] - COURANT * (ey_x[x][t] - ey[x][t] - (ex_y[t] - ex[x][t])) for t in every]
                if step == 0:
                    next_y = [ahead_y1[part][t] + half_next[t] * hz[-1][t] for t in every]
                    next_z = [ahead_z1[part][t] - half_next[t] * hy[-1][t] for t in every]
                for x in layers:
                    hz_y, hx_y = shifts.y_down(hz[x]), shifts.y_down(hx[x])
                    span = every if step == 0 else own
                    if x > 0:
                        hy_x, hz_x = hy[x - 1], hz[x - 1]
                    elif step == 0:
                        hy_x, hz_x = below_y, below_z
                    else:
                        hy_x, hz_x = None, None
                    new_x, new_y, new_z = [], [], []
                    for t in span:
                        diff_y = hz[x][t] if hz_x is None else hz[x][t] - hz_x[t]
                        diff_z = hy[x][t] if hy_x is None else hy[x][t] - hy_x[t]
                        new_x.append(ex[x][t] + half[x][t] * (hz[x][t] - hz_y[t] - (hy[x][t] - shifts.z_down(hy[x][t]))))
                        new_y.append(ey[x][t] + half[x][t] * (hx[x][t] - shifts.z_down(hx[x][t]) - diff_y))
                        new_z.append(
                            ez[x][t] + half[x][t] * (diff_z - (hx[x][t] - hx_y[t])) + sources[step][x][part][t]
                        )
                    ex[x], ey[x], ez[x] = new_x, new_y, new_z
                if step == 0:
                    kept_one[run, part] = (list(ex), list(ey), list(ez))
                    kept_next[run, part] = (next_y, next_z)
                else:
                    kept_two[run, part] = (ex, ey, ez)
                    kept_high[run, part] = (hy[-1], hz[-1])

    for t in own:
        for x in layers:
            total = None
            for comp in range(3):
                for now, later in ((kept_one, kept_two), (kept_two, kept_one)):
                    term = (
                        now[0, 0][comp][x][t] * later[1, 0][comp][x][t] - now[0, 1][comp][x][t] * later[1, 1][comp][x][t]
                    )
                    total = term if total is None else total + term
            cross_ref[local.rows(x, t), :] = total
        total = None
        for run in range(2):
            for which, sign in ((0, 1.0), (1, -1.0)):
                term = (
                    kept_next[run, 0][which][t] * kept_high[1 - run, 0][1 - which][t]
                    - kept_next[run, 1][which][t] * kept_high[1 - run, 1][1 - which][t]
                )
                term = term if sign > 0 else -term
                total = term if total is None else total + term
        share_ref[t * nz:(t + 1) * nz, :] = half_next[t] * total


def last_kernel(dims, material_ref, table_ref, cross_ref, other_ref, same_share_ref, other_share_ref, out_ref):
    nz, width_x, tiles = dims
    local = Local(dims, None, None, table_ref, material_ref, None, None)
    for x in range(width_x):
        for t in range(tiles):
            rows = local.rows(x, t)
            total = cross_ref[rows, :] + other_ref[rows, :]
            if x == 0:
                span = slice(t * nz, (t + 1) * nz)
                total = total + (same_share_ref[span, :] + other_share_ref[span, :])
            out_ref[rows, :] = -COURANT * inverse_eps(material_ref[rows, :], table_ref) * total


VMEM = pl.BlockSpec(memory_space=pltpu.VMEM)
SMEM = pl.BlockSpec(memory_space=pltpu.SMEM)


def call(kernel, name, in_specs, shapes, cost, scratch=()):
    return pl.pallas_call(
        kernel,
        name=name,
        out_shape=[jax.ShapeDtypeStruct(shape, jnp.float32) for shape in shapes],
        in_specs=in_specs,
        out_specs=[VMEM] * len(shapes),
        scratch_shapes=list(scratch),
        compiler_params=pltpu.CompilerParams(vmem_limit_bytes=48 * 1024 * 1024),
        cost_estimate=pl.CostEstimate(flops=cost, bytes_accessed=cost, transcendentals=0),
    )


def moved(value, axis, steps):
    count = lax.axis_size(axis)
    return lax.ppermute(value, axis, [(source, (source + steps) % count) for source in range(count)])


def local(field_state, material_map, eps_table, bloch_phase, source_cells, source_wave):
    nz, width_x, width_y = material_map.shape
    tiles = width_y // LANES
    dims = (nz, width_x, tiles)
    rows = nz * tiles * width_x
    fields = field_state.reshape(24, nz, width_x, tiles, LANES).transpose(0, 1, 3, 2, 4).reshape(24, rows, LANES)
    material = material_map.reshape(nz, width_x, tiles, LANES).transpose(0, 2, 1, 3).reshape(rows, LANES)
    cells = source_cells.reshape(2)
    wave = source_wave.reshape(8)
    unit = nz * tiles
    two = lax.axis_size("gy") == 2
    count_x, count_src = lax.axis_size("gx"), lax.axis_size("src")

    face, edge = call(
        functools.partial(first_kernel, dims), "faces", [VMEM, VMEM, SMEM],
        [(8 * unit, LANES), (width_x * nz, LANES)], 2_000_000,
    )(fields, material, eps_table)
    face = moved(face, "gx", -1)
    below = moved(edge, "gy", 1)
    above = below if two else moved(edge, "gy", -1)
    scratch = (pltpu.VMEM((width_x * nz, LANES), jnp.float32),)
    down, up = call(
        functools.partial(second_kernel, dims, two), "partials", [VMEM, VMEM, SMEM, SMEM, SMEM, SMEM, VMEM, VMEM],
        [(9 * unit + nz, LANES), (8 * unit + nz, LANES)], 4_000_000, scratch,
    )(fields, material, eps_table, bloch_phase, cells, wave, below, above)
    down = moved(down, "gx", -1)
    up = moved(up, "gx", 1)
    cross, share = call(
        functools.partial(third_kernel, dims, two), "steps",
        [VMEM, VMEM, SMEM, SMEM, SMEM, SMEM, VMEM, VMEM, VMEM, VMEM, VMEM],
        [(rows, LANES), (unit, LANES)], 8_000_000, scratch,
    )(fields, material, eps_table, bloch_phase, cells, wave, below, above, face, down, up)
    same_share = moved(share, "gx", 1)
    other_share = lax.ppermute(
        share, ("gx", "src"),
        [
            (x * count_src + s, ((x + 1) % count_x) * count_src + (s + 1) % count_src)
            for x in range(count_x)
            for s in range(count_src)
        ],
    )
    other = moved(cross, "src", 1)
    (out,) = call(
        functools.partial(last_kernel, dims), "gradient", [VMEM, SMEM, VMEM, VMEM, VMEM, VMEM],
        [(rows, LANES)], 500_000,
    )(material, eps_table, cross, other, same_share, other_share)
    return out.reshape(nz, tiles, width_x, LANES).transpose(0, 2, 1, 3).reshape(nz, width_x, width_y)


def solution(mesh):
    return jax.shard_map(
        local,
        mesh=mesh,
        in_specs=(
            P(("design", "src"), None, None, None, None, "gx", "gy"),
            P("design", "gx", "gy"),
            P(),
            P("design"),
            P(("design", "src"), None),
            P(("design", "src"), None, None, None),
        ),
        out_specs=P("design", "gx", "gy"),
        check_vma=False,
    )
```

```python
import functools

import jax
import jax.numpy as jnp
from jax import lax
from jax.experimental import pallas as pl
from jax.experimental.pallas import tpu as pltpu
from jax.sharding import PartitionSpec as P

COURANT = 0.5
LANES = 128
EDGE = 4


def lane_iota(nz):
    return lax.broadcasted_iota(jnp.int32, (nz, LANES), 1)


def row_iota(nz):
    return lax.broadcasted_iota(jnp.int32, (nz, LANES), 0)


def pack_edges(values, lane):
    packed = jnp.zeros_like(values[0])
    for spot, value in enumerate(values):
        moved = pltpu.roll(value, EDGE * spot + 2, 1)
        packed = jnp.where(lane // EDGE == spot, moved, packed)
    return packed


def unpack_edge(packed, spot):
    return pltpu.roll(packed, LANES - EDGE * spot - 2, 1)


class Shifts:
    def __init__(self, nz):
        self.nz = nz
        self.row = row_iota(nz)
        self.lane = lane_iota(nz)

    def z_up(self, value):
        return jnp.where(self.row == self.nz - 1, 0.0, pltpu.roll(value, self.nz - 1, 0))

    def z_down(self, value):
        return jnp.where(self.row == 0, 0.0, pltpu.roll(value, 1, 0))

    def y_up(self, tiles):
        moved = [pltpu.roll(value, LANES - 1, 1) for value in tiles]
        count = len(tiles)
        return [jnp.where(self.lane == LANES - 1, moved[(t + 1) % count], moved[t]) for t in range(count)]

    def y_down(self, tiles):
        moved = [pltpu.roll(value, 1, 1) for value in tiles]
        count = len(tiles)
        return [jnp.where(self.lane == 0, moved[(t - 1) % count], moved[t]) for t in range(count)]


def turn(real_part, imag_part, cosine, sine):
    return real_part * cosine - imag_part * sine, real_part * sine + imag_part * cosine


def phases(phase_ref):
    row = lax.broadcasted_iota(jnp.int32, (8, LANES), 0)
    angle = jnp.where(row == 0, phase_ref[0], phase_ref[1])
    cosine, sine = jnp.cos(angle), jnp.sin(angle)
    return cosine[0:1], sine[0:1], cosine[1:2], sine[1:2]


def y_turn(cosine_y, sine_y, lane):
    first = lax.axis_index("gy") == 0
    last = lax.axis_index("gy") == lax.axis_size("gy") - 1
    upper = lane < LANES // 2
    cosine = jnp.where(upper, jnp.where(last, cosine_y, 1.0), jnp.where(first, cosine_y, 1.0))
    return cosine, jnp.where(upper, jnp.where(last, sine_y, 0.0), jnp.where(first, -sine_y, 0.0))


def inverse_eps(material, table_ref):
    level = jnp.full(material.shape, table_ref[0], jnp.float32)
    for index in range(1, table_ref.shape[0]):
        level = jnp.where(material == index, table_ref[index], level)
    return 1.0 / level


def spot_of(run, part, comp):
    return (run * 2 + part) * 6 + comp


class Local:
    def __init__(self, dims, field_ref, edge_ref, table_ref, material_ref, cells_ref, wave_ref):
        self.nz, self.width_x, self.tiles = dims
        self.field_ref, self.edge_ref = field_ref, edge_ref
        self.table_ref, self.material_ref = table_ref, material_ref
        self.cells_ref, self.wave_ref = cells_ref, wave_ref
        self.shifts = Shifts(self.nz)

    def rows(self, x, t):
        return pl.ds(t * self.width_x + x, self.nz, stride=self.tiles * self.width_x)

    def own(self, run, part, comp, x, t):
        return self.field_ref[spot_of(run, part, comp), self.rows(x, t), :]

    def edge(self, x):
        return self.edge_ref[x * self.nz:(x + 1) * self.nz, :]

    def load(self, run, comp, x, turn_y):
        cosine, sine = turn_y
        packed = self.edge(x)
        parts = [[self.own(run, part, comp, x, t) for t in range(self.tiles)] for part in range(2)]
        edges = [unpack_edge(packed, spot_of(run, part, comp)) for part in range(2)]
        edges = turn(edges[0], edges[1], cosine, sine if run == 0 else -sine)
        return [parts[part] + [edges[part]] for part in range(2)]

    def eps(self, x):
        own = [inverse_eps(self.material_ref[self.rows(x, t), :], self.table_ref) for t in range(self.tiles)]
        return own + [inverse_eps(unpack_edge(self.edge(x), 24), self.table_ref)]

    def hits(self, run, x):
        total_x = self.width_x * lax.axis_size("gx")
        width_y = self.tiles * LANES
        total_y = width_y * lax.axis_size("gy")
        begin_y = lax.axis_index("gy") * width_y
        plane = self.shifts.row * total_x + lax.axis_index("gx") * self.width_x + x
        masks = []
        for t in range(self.tiles + 1):
            lane = self.shifts.lane
            if t < self.tiles:
                column = begin_y + t * LANES + lane
            else:
                column = begin_y + jnp.where(lane < LANES // 2, lane + width_y, lane - LANES)
                column = jnp.where(column < 0, column + total_y, column)
                column = jnp.where(column >= total_y, column - total_y, column)
            masks.append(plane * total_y + column == self.cells_ref[run])
        return masks

    def source(self, run, step, masks, turn_y):
        cosine, sine = turn_y
        amplitude = [self.wave_ref[(run * 2 + part) * 2 + step] for part in range(2)]
        turned = turn(amplitude[0], amplitude[1], cosine, sine if run == 0 else -sine)
        return [
            [jnp.where(mask, amplitude[part] if t < self.tiles else turned[part], 0.0) for t, mask in enumerate(masks)]
            for part in range(2)
        ]


def face_kernel(dims, field_ref, material_ref, face_ref, planes_ref, layer_ref, sems):
    nz, width_x, tiles = dims
    copies = [
        pltpu.make_async_copy(field_ref.at[pl.ds(6 * pair + 1, 2)], planes_ref.at[pair], sems.at[pair])
        for pair in range(4)
    ]
    copies.append(pltpu.make_async_copy(material_ref, layer_ref, sems.at[4]))
    for copy in copies:
        copy.start()
    for pair in range(4):
        copies[pair].wait()
        for which in range(2):
            for t in range(tiles):
                at = ((pair * 2 + which) * tiles + t) * nz
                face_ref[at:at + nz, :] = planes_ref[pair, which, pl.ds(t * width_x, nz, stride=tiles * width_x), :]
    copies[4].wait()
    for t in range(tiles):
        at = (8 * tiles + t) * nz
        face_ref[at:at + nz, :] = layer_ref[pl.ds(t * width_x, nz, stride=tiles * width_x), :].astype(jnp.float32)


def edge_kernel(dims, field_ref, material_ref, edge_ref):
    nz, width_x, tiles = dims
    local = Local(dims, field_ref, None, None, material_ref, None, None)
    lane = lane_iota(nz)
    for x in range(width_x):
        values = []
        for run in range(2):
            for part in range(2):
                for comp in range(6):
                    values.append(
                        jnp.where(
                            lane < LANES // 2,
                            local.own(run, part, comp, x, 0),
                            local.own(run, part, comp, x, tiles - 1),
                        )
                    )
        material = jnp.where(
            lane < LANES // 2, material_ref[local.rows(x, 0), :], material_ref[local.rows(x, tiles - 1), :]
        )
        values.append(material.astype(jnp.float32))
        edge_ref[x * nz:(x + 1) * nz, :] = pack_edges(values, lane)


def merged_edges(below_ref, above_ref, edge_ref):
    if above_ref is None:
        return below_ref
    lane = lax.broadcasted_iota(jnp.int32, below_ref.shape, 1)
    edge_ref[...] = jnp.where(lane % EDGE < 2, below_ref[...], above_ref[...])
    return edge_ref


def small_steps(local, ex, ey, ez, hx, hy, hz, ey_x, ez_x):
    shifts = local.shifts
    every = range(len(ex))
    ez_y, ex_y = shifts.y_up(ez), shifts.y_up(ex)
    new_x = None
    if hx is not None:
        new_x = [hx[t] - COURANT * (ez_y[t] - ez[t] - (shifts.z_up(ey[t]) - ey[t])) for t in every]
    diff_z = [-ez[t] if ez_x is None else ez_x[t] - ez[t] for t in every]
    diff_y = [-ey[t] if ey_x is None else ey_x[t] - ey[t] for t in every]
    new_y = [hy[t] - COURANT * (shifts.z_up(ex[t]) - ex[t] - diff_z[t]) for t in every]
    new_z = [hz[t] - COURANT * (diff_y[t] - (ex_y[t] - ex[t])) for t in every]
    return new_x, new_y, new_z


def grown(local, ex, ey, ez, hx, hy, hz, hy_x, hz_x, half, source, count):
    shifts = local.shifts
    hz_y, hx_y = shifts.y_down(hz), shifts.y_down(hx)
    new_x, new_y, new_z = [], [], []
    for t in range(count):
        diff_y = hz[t] if hz_x is None else hz[t] - hz_x[t]
        diff_z = hy[t] if hy_x is None else hy[t] - hy_x[t]
        if ex is not None:
            new_x.append(ex[t] + half[t] * (hz[t] - hz_y[t] - (hy[t] - shifts.z_down(hy[t]))))
        new_y.append(ey[t] + half[t] * (hx[t] - shifts.z_down(hx[t]) - diff_y))
        new_z.append(ez[t] + half[t] * (diff_z - (hx[t] - hx_y[t])) + source[t])
    return new_x, new_y, new_z


def started(dims, two, field_ref, material_ref, table_ref, phase_ref, cells_ref, wave_ref, below_ref, above_ref, edge_ref):
    edges = merged_edges(below_ref, None if two else above_ref, edge_ref)
    local = Local(dims, field_ref, edges, table_ref, material_ref, cells_ref, wave_ref)
    cosine_x, sine_x, cosine_y, sine_y = phases(phase_ref)
    first = lax.axis_index("gx") == 0
    last = lax.axis_index("gx") == lax.axis_size("gx") - 1
    ahead = (jnp.where(last, cosine_x, 1.0), jnp.where(last, sine_x, 0.0))
    back = (jnp.where(first, cosine_x, 1.0), jnp.where(first, -sine_x, 0.0))
    return local, y_turn(cosine_y, sine_y, local.shifts.lane), ahead, back


def store_tiles(ref, unit, values, tiles, nz):
    for t in range(tiles):
        at = (unit * tiles + t) * nz
        ref[at:at + nz, :] = values[t]


def lower_kernel(dims, two, *refs):
    nz, _, tiles = dims
    *given, down_ref, edge_ref = refs
    local, turn_y, _, _ = started(dims, two, *given, edge_ref)
    half = [COURANT * value for value in local.eps(0)]
    edges = [None] * 17
    for run in range(2):
        low = [local.load(run, comp, 0, turn_y) for comp in range(6)]
        nearer = [local.load(run, comp, 1, turn_y) for comp in (1, 2)]
        source = local.source(run, 0, local.hits(run, 0), turn_y)
        for part in range(2):
            ex, ey, ez, hx, hy, hz = [low[comp][part] for comp in range(6)]
            hx, hy, hz = small_steps(local, ex, ey, ez, hx, hy, hz, nearer[0][part], nearer[1][part])
            _, new_y, new_z = grown(local, None, ey, ez, hx, hy, hz, None, None, half, source[part], tiles + 1)
            for which, value, initial in ((0, new_y, ey), (1, new_z, ez)):
                unit = (run * 2 + part) * 2 + which
                store_tiles(down_ref, unit, value, tiles, nz)
                edges[unit] = initial[tiles]
                edges[8 + unit] = value[tiles]
    edges[16] = unpack_edge(local.edge(0), 24)
    at = 8 * tiles * nz
    down_ref[at:at + nz, :] = pack_edges(edges, local.shifts.lane)


def upper_kernel(dims, two, *refs):
    nz, width_x, tiles = dims
    *given, up_ref, edge_ref = refs
    local, turn_y, _, _ = started(dims, two, *given, edge_ref)
    edges = []
    for run in range(2):
        high = [local.load(run, comp, width_x - 1, turn_y) for comp in (0, 1, 2, 4, 5)]
        for part in range(2):
            ex, ey, ez, hy, hz = [values[part] for values in high]
            _, hy, hz = small_steps(local, ex, ey, ez, None, hy, hz, None, None)
            for which, value in ((0, hy), (1, hz)):
                store_tiles(up_ref, (run * 2 + part) * 2 + which, value, tiles, nz)
                edges.append(value[tiles])
    at = 8 * tiles * nz
    up_ref[at:at + nz, :] = pack_edges(edges, local.shifts.lane)


def halo(dims, ref, edge, first_spot, run, which, angle):
    nz, _, tiles = dims
    cosine, sine = angle
    units = [(run * 2 + part) * 2 + which for part in range(2)]
    values = [
        [ref[(unit * tiles + t) * nz:(unit * tiles + t + 1) * nz, :] for t in range(tiles)]
        + [unpack_edge(edge, first_spot + unit)]
        for unit in units
    ]
    signed = sine if run == 0 else -sine
    turned = [turn(values[0][t], values[1][t], cosine, signed) for t in range(tiles + 1)]
    return [[value[part] for value in turned] for part in range(2)]


def eps_above(local, face_ref, edge):
    nz, tiles = local.nz, local.tiles
    own = [face_ref[(8 * tiles + t) * nz:(8 * tiles + t + 1) * nz, :] for t in range(tiles)]
    return [inverse_eps(value, local.table_ref) for value in own + [unpack_edge(edge, 16)]]


def share_kernel(dims, two, *refs):
    nz, width_x, tiles = dims
    *given, face_ref, down_ref, share_ref, edge_ref = refs
    local, turn_y, ahead, _ = started(dims, two, *given, edge_ref)
    edge = down_ref[8 * tiles * nz:(8 * tiles + 1) * nz, :]
    half = [COURANT * value for value in local.eps(width_x - 1)]
    half_above = [COURANT * value for value in eps_above(local, face_ref, edge)]
    kept_e, kept_h = {}, {}
    every = range(tiles + 1)
    for run in range(2):
        low = [local.load(run, comp, width_x - 2, turn_y) for comp in range(6)]
        high = [local.load(run, comp, width_x - 1, turn_y) for comp in range(6)]
        source = local.source(run, 0, local.hits(run, width_x - 1), turn_y)
        early = [halo(dims, face_ref, edge, 0, run, which, ahead) for which in range(2)]
        later = [halo(dims, down_ref, edge, 8, run, which, ahead) for which in range(2)]
        for part in range(2):
            ex, ey, ez, hx, hy, hz = [high[comp][part] for comp in range(6)]
            low_x, low_y, low_z, _, low_hy, low_hz = [low[comp][part] for comp in range(6)]
            _, low_hy, low_hz = small_steps(local, low_x, low_y, low_z, None, low_hy, low_hz, ey, ez)
            hx, hy, hz = small_steps(local, ex, ey, ez, hx, hy, hz, early[0][part], early[1][part])
            ex, ey, ez = grown(local, ex, ey, ez, hx, hy, hz, low_hy, low_hz, half, source[part], tiles + 1)
            above_y = [later[0][part][t] + half_above[t] * hz[t] for t in every]
            above_z = [later[1][part][t] - half_above[t] * hy[t] for t in every]
            _, hy, hz = small_steps(local, ex, ey, ez, None, hy, hz, above_y, above_z)
            kept_e[run, part] = (above_y, above_z)
            kept_h[run, part] = (hy, hz)
    for t in range(tiles):
        total = 0.0
        for run in range(2):
            for which, sign in ((0, 1.0), (1, -1.0)):
                term = (
                    kept_e[run, 0][which][t] * kept_h[1 - run, 0][1 - which][t]
                    - kept_e[run, 1][which][t] * kept_h[1 - run, 1][1 - which][t]
                )
                total = total + sign * term
        share_ref[t * nz:(t + 1) * nz, :] = half_above[t] * total


def steps_kernel(dims, two, *refs):
    nz, width_x, tiles = dims
    *given, face_ref, down_ref, up_ref, share_ref, cross_ref, edge_ref = refs
    local, turn_y, ahead, back = started(dims, two, *given, edge_ref)
    every, own, layers = range(tiles + 1), range(tiles), range(width_x)
    down_edge = down_ref[8 * tiles * nz:(8 * tiles + 1) * nz, :]
    up_edge = up_ref[8 * tiles * nz:(8 * tiles + 1) * nz, :]
    half = [[COURANT * value for value in local.eps(x)] for x in layers]
    half_above = [COURANT * value for value in eps_above(local, face_ref, down_edge)]
    kept_one, kept_two = {}, {}
    for run in range(2):
        masks = [local.hits(run, x) for x in layers]
        sources = [[local.source(run, step, masks[x], turn_y) for x in layers] for step in range(2)]
        fields = [[local.load(run, comp, x, turn_y) for x in layers] for comp in range(6)]
        early = [halo(dims, face_ref, down_edge, 0, run, which, ahead) for which in range(2)]
        later = [halo(dims, down_ref, down_edge, 8, run, which, ahead) for which in range(2)]
        under = [halo(dims, up_ref, up_edge, 0, run, which, back) for which in range(2)]
        for part in range(2):
            ex, ey, ez, hx, hy, hz = [[fields[comp][x][part] for x in layers] for comp in range(6)]
            under_y = [under[0][part][t] + COURANT * ez[0][t] for t in every]
            under_z = [under[1][part][t] - COURANT * ey[0][t] for t in every]
            above_y, above_z = early[0][part], early[1][part]
            for step in range(2):
                ey_x, ez_x = ey[1:] + [above_y], ez[1:] + [above_z]
                for x in layers:
                    hx[x], hy[x], hz[x] = small_steps(
                        local, ex[x], ey[x], ez[x], hx[x], hy[x], hz[x], ey_x[x], ez_x[x]
                    )
                if step == 0:
                    above_y = [later[0][part][t] + half_above[t] * hz[-1][t] for t in every]
                    above_z = [later[1][part][t] - half_above[t] * hy[-1][t] for t in every]
                else:
                    under_y, under_z = None, None
                for x in layers:
                    hy_x, hz_x = (under_y, under_z) if x == 0 else (hy[x - 1], hz[x - 1])
                    ex[x], ey[x], ez[x] = grown(
                        local, ex[x], ey[x], ez[x], hx[x], hy[x], hz[x], hy_x, hz_x, half[x], sources[step][x][part],
                        tiles if step else tiles + 1,
                    )
                (kept_two if step else kept_one)[run, part] = (list(ex), list(ey), list(ez))
    for t in own:
        for x in layers:
            total = share_ref[t * nz:(t + 1) * nz, :] if x == 0 else 0.0
            for comp in range(3):
                for now, later in ((kept_one, kept_two), (kept_two, kept_one)):
                    total = total + (
                        now[0, 0][comp][x][t] * later[1, 0][comp][x][t] - now[0, 1][comp][x][t] * later[1, 1][comp][x][t]
                    )
            cross_ref[local.rows(x, t), :] = -half[x][t] * total


def sum_kernel(own_ref, other_ref, out_ref):
    out_ref[...] = own_ref[...] + other_ref[...]


VMEM = pl.BlockSpec(memory_space=pltpu.VMEM)
SMEM = pl.BlockSpec(memory_space=pltpu.SMEM)


ANY = pl.BlockSpec(memory_space=pltpu.HBM)


def call(kernel, name, in_specs, rows, cost, scratch=()):
    return pl.pallas_call(
        kernel,
        name=name,
        out_shape=jax.ShapeDtypeStruct((rows, LANES), jnp.float32),
        in_specs=in_specs,
        out_specs=VMEM,
        scratch_shapes=list(scratch),
        compiler_params=pltpu.CompilerParams(vmem_limit_bytes=48 * 1024 * 1024),
        cost_estimate=pl.CostEstimate(flops=0, bytes_accessed=cost, transcendentals=0),
    )


def moved(value, axis, steps):
    count = lax.axis_size(axis)
    return lax.ppermute(value, axis, [(source, (source + steps) % count) for source in range(count)])


def local(field_state, material_map, eps_table, bloch_phase, source_cells, source_wave):
    nz, width_x, width_y = material_map.shape
    tiles = width_y // LANES
    dims = (nz, width_x, tiles)
    rows = nz * tiles * width_x
    fields = field_state.reshape(24, nz, width_x, tiles, LANES).transpose(0, 1, 3, 2, 4).reshape(24, rows, LANES)
    material = material_map.reshape(nz, width_x, tiles, LANES).transpose(0, 2, 1, 3).reshape(rows, LANES)
    cells = source_cells.reshape(2)
    wave = source_wave.reshape(8)
    unit = nz * tiles
    two = lax.axis_size("gy") == 2

    face = call(
        functools.partial(face_kernel, dims), "faces", [ANY, ANY], 9 * unit, 1_000_000,
        (
            pltpu.VMEM((4, 2, rows, LANES), jnp.float32),
            pltpu.VMEM((rows, LANES), jnp.int32),
            pltpu.SemaphoreType.DMA((5,)),
        ),
    )(fields, material)
    face = moved(face, "gx", -1)
    edge = call(functools.partial(edge_kernel, dims), "edges", [VMEM, VMEM], width_x * nz, 20_000_000)(fields, material)
    below = moved(edge, "gy", 1)
    above = below if two else moved(edge, "gy", -1)
    given = (fields, material, eps_table, bloch_phase, cells, wave, below, above)
    specs = [VMEM, VMEM, SMEM, SMEM, SMEM, SMEM, VMEM, VMEM]
    scratch = (pltpu.VMEM((width_x * nz, LANES), jnp.float32),)
    down = call(functools.partial(lower_kernel, dims, two), "lower", specs, 8 * unit + nz, 20_000_000, scratch)(*given)
    down = moved(down, "gx", -1)
    up = call(functools.partial(upper_kernel, dims, two), "upper", specs, 8 * unit + nz, 20_000_000, scratch)(*given)
    up = moved(up, "gx", 1)
    share = call(
        functools.partial(share_kernel, dims, two), "share", specs + [VMEM] * 2, unit, 20_000_000, scratch
    )(*given, face, down)
    share = moved(share, "gx", 1)
    cross = call(
        functools.partial(steps_kernel, dims, two), "steps", specs + [VMEM] * 4, rows, 20_000_000, scratch
    )(*given, face, down, up, share)
    other = moved(cross, "src", 1)
    out = call(sum_kernel, "gradient", [VMEM, VMEM], rows, 500_000)(cross, other)
    return out.reshape(nz, tiles, width_x, LANES).transpose(0, 2, 1, 3).reshape(nz, width_x, width_y)


def solution(mesh):
    return jax.shard_map(
        local,
        mesh=mesh,
        in_specs=(
            P(("design", "src"), None, None, None, None, "gx", "gy"),
            P("design", "gx", "gy"),
            P(),
            P("design"),
            P(("design", "src"), None),
            P(("design", "src"), None, None, None),
        ),
        out_specs=P("design", "gx", "gy"),
        check_vma=False,
    )
```

```python
import functools

import jax
import jax.numpy as jnp
from jax import lax
from jax.experimental import pallas as pl
from jax.experimental.pallas import tpu as pltpu
from jax.sharding import PartitionSpec as P

COURANT = 0.5
LANES = 128
EDGE = 4


def lane_iota(nz):
    return lax.broadcasted_iota(jnp.int32, (nz, LANES), 1)


def row_iota(nz):
    return lax.broadcasted_iota(jnp.int32, (nz, LANES), 0)


def pack_edges(values, lane):
    packed = jnp.zeros_like(values[0])
    for spot, value in enumerate(values):
        moved = pltpu.roll(value, EDGE * spot + 2, 1)
        packed = jnp.where(lane // EDGE == spot, moved, packed)
    return packed


def unpack_edge(packed, spot):
    return pltpu.roll(packed, LANES - EDGE * spot - 2, 1)


class Shifts:
    def __init__(self, nz):
        self.nz = nz
        self.row = row_iota(nz)
        self.lane = lane_iota(nz)

    def z_up(self, value):
        return jnp.where(self.row == self.nz - 1, 0.0, pltpu.roll(value, self.nz - 1, 0))

    def z_down(self, value):
        return jnp.where(self.row == 0, 0.0, pltpu.roll(value, 1, 0))

    def y_up(self, tiles):
        moved = [pltpu.roll(value, LANES - 1, 1) for value in tiles]
        count = len(tiles)
        return [jnp.where(self.lane == LANES - 1, moved[(t + 1) % count], moved[t]) for t in range(count)]

    def y_down(self, tiles):
        moved = [pltpu.roll(value, 1, 1) for value in tiles]
        count = len(tiles)
        return [jnp.where(self.lane == 0, moved[(t - 1) % count], moved[t]) for t in range(count)]


def turn(real_part, imag_part, cosine, sine):
    return real_part * cosine - imag_part * sine, real_part * sine + imag_part * cosine


def inverse_eps(material, levels):
    level = levels[0]
    for index in range(1, len(levels)):
        level = jnp.where(material == index, levels[index], level)
    return 1.0 / level


AHEAD, BACK, EDGES, WAVE, TURNED, LEVELS = 0, 2, 4, 8, 16, 24


def spot_of(run, part, comp):
    return (run * 2 + part) * 6 + comp


class Local:
    def __init__(self, dims, field_ref, edge_ref, small_ref, half_ref, mask_ref):
        self.nz, self.width_x, self.tiles = dims
        self.field_ref, self.edge_ref = field_ref, edge_ref
        self.small_ref, self.half_ref, self.mask_ref = small_ref, half_ref, mask_ref
        self.shifts = Shifts(self.nz)

    def rows(self, x, t):
        return pl.ds(t * self.width_x + x, self.nz, stride=self.tiles * self.width_x)

    def own(self, run, part, comp, x, t):
        return self.field_ref[spot_of(run, part, comp), self.rows(x, t), :]

    def edge(self, x):
        return self.edge_ref[x * self.nz:(x + 1) * self.nz, :]

    def small(self, row):
        return self.small_ref[row:row + 1, :]

    def angle(self, row, run):
        sine = self.small(row + 1)
        return self.small(row), sine if run == 0 else -sine

    def levels(self):
        return [self.small(row) for row in range(LEVELS, self.small_ref.shape[0])]

    def load(self, run, comp, x):
        packed = self.edge(x)
        parts = [[self.own(run, part, comp, x, t) for t in range(self.tiles)] for part in range(2)]
        edges = [unpack_edge(packed, spot_of(run, part, comp)) for part in range(2)]
        edges = turn(edges[0], edges[1], *self.angle(EDGES, run))
        return [parts[part] + [edges[part]] for part in range(2)]

    def half(self, x):
        starts = [(x * self.tiles + t) * self.nz for t in range(self.tiles)]
        own = [self.half_ref[at:at + self.nz, :] for at in starts]
        return own + [COURANT * inverse_eps(unpack_edge(self.edge(x), 24), self.levels())]

    def source(self, run, step, x):
        parts = []
        for part in range(2):
            values = []
            for t in range(self.tiles + 1):
                at = ((run * self.width_x + x) * (self.tiles + 1) + t) * self.nz
                row = (WAVE if t < self.tiles else TURNED) + (run * 2 + part) * 2 + step
                values.append(self.mask_ref[at:at + self.nz, :] * self.small(row))
            parts.append(values)
        return parts


def face_kernel(dims, field_hbm, face_ref, planes_ref, sems):
    nz, width_x, tiles = dims
    copies = [
        pltpu.make_async_copy(field_hbm.at[pl.ds(6 * pair + 1, 2)], planes_ref.at[pair], sems.at[pair])
        for pair in range(4)
    ]
    for copy in copies:
        copy.start()
    for pair in range(4):
        copies[pair].wait()
        for which in range(2):
            values = [planes_ref[pair, which, pl.ds(t * width_x, nz, stride=tiles * width_x), :] for t in range(tiles)]
            store_tiles(face_ref, pair * 2 + which, values, tiles, nz)


def edge_kernel(dims, order_ref, field_ref, material_ref, edge_ref):
    nz, width_x, tiles = dims
    local = Local(dims, field_ref, None, None, None, None)
    lane = lane_iota(nz)
    for x in range(width_x):
        values = []
        for run in range(2):
            for part in range(2):
                for comp in range(6):
                    values.append(
                        jnp.where(
                            lane < LANES // 2,
                            local.own(run, part, comp, x, 0),
                            local.own(run, part, comp, x, tiles - 1),
                        )
                    )
        material = jnp.where(
            lane < LANES // 2, material_ref[local.rows(x, 0), :], material_ref[local.rows(x, tiles - 1), :]
        )
        values.append(material.astype(jnp.float32))
        edge_ref[x * nz:(x + 1) * nz, :] = pack_edges(values, lane)


def prepare_kernel(
    dims, order_ref, material_ref, table_ref, phase_ref, cells_ref, wave_ref, small_ref, half_ref, mask_ref,
):
    nz, width_x, tiles = dims
    row = lax.broadcasted_iota(jnp.int32, (8, LANES), 0)
    angle = jnp.where(row == 0, phase_ref[0], phase_ref[1])
    cosine, sine = jnp.cos(angle), jnp.sin(angle)
    cosine_x, sine_x, cosine_y, sine_y = cosine[0:1], sine[0:1], cosine[1:2], sine[1:2]
    first_x, first_y = lax.axis_index("gx") == 0, lax.axis_index("gy") == 0
    last_x = lax.axis_index("gx") == lax.axis_size("gx") - 1
    last_y = lax.axis_index("gy") == lax.axis_size("gy") - 1
    small_ref[AHEAD:AHEAD + 1, :] = jnp.where(last_x, cosine_x, 1.0)
    small_ref[AHEAD + 1:AHEAD + 2, :] = jnp.where(last_x, sine_x, 0.0)
    small_ref[BACK:BACK + 1, :] = jnp.where(first_x, cosine_x, 1.0)
    small_ref[BACK + 1:BACK + 2, :] = jnp.where(first_x, -sine_x, 0.0)
    upper = lax.broadcasted_iota(jnp.int32, (1, LANES), 1) < LANES // 2
    cosine = jnp.where(upper, jnp.where(last_y, cosine_y, 1.0), jnp.where(first_y, cosine_y, 1.0))
    sine = jnp.where(upper, jnp.where(last_y, sine_y, 0.0), jnp.where(first_y, -sine_y, 0.0))
    small_ref[EDGES:EDGES + 1, :] = cosine
    small_ref[EDGES + 1:EDGES + 2, :] = sine
    small_ref[EDGES + 2:WAVE, :] = jnp.zeros((WAVE - EDGES - 2, LANES), jnp.float32)
    for run in range(2):
        for step in range(2):
            spots = [(run * 2 + part) * 2 + step for part in range(2)]
            amplitude = [wave_ref[0, run, part, step] for part in range(2)]
            turned = turn(amplitude[0], amplitude[1], cosine, sine if run == 0 else -sine)
            for part in range(2):
                row = WAVE + spots[part]
                small_ref[row:row + 1, :] = jnp.full((1, LANES), amplitude[part], jnp.float32)
                row = TURNED + spots[part]
                small_ref[row:row + 1, :] = turned[part]
    for index in range(table_ref.shape[0]):
        small_ref[LEVELS + index:LEVELS + index + 1, :] = jnp.full((1, LANES), table_ref[index], jnp.float32)
    levels = [table_ref[index] for index in range(table_ref.shape[0])]
    total_x = width_x * lax.axis_size("gx")
    width_y = tiles * LANES
    total_y = width_y * lax.axis_size("gy")
    begin_y = lax.axis_index("gy") * width_y
    z, lane = row_iota(nz), lane_iota(nz)
    for x in range(width_x):
        plane = z * total_x + lax.axis_index("gx") * width_x + x
        for t in range(tiles + 1):
            if t < tiles:
                column = begin_y + t * LANES + lane
                material = material_ref[pl.ds(t * width_x + x, nz, stride=tiles * width_x), :]
                at = (x * tiles + t) * nz
                half_ref[at:at + nz, :] = COURANT * inverse_eps(material, levels)
            else:
                column = begin_y + jnp.where(lane < LANES // 2, lane + width_y, lane - LANES)
                column = jnp.where(column < 0, column + total_y, column)
                column = jnp.where(column >= total_y, column - total_y, column)
            index = plane * total_y + column
            for run in range(2):
                at = ((run * width_x + x) * (tiles + 1) + t) * nz
                mask_ref[at:at + nz, :] = jnp.where(index == cells_ref[0, run], 1.0, 0.0)


def merged_edges(below_ref, above_ref, edge_ref):
    if above_ref is None:
        return below_ref
    lane = lax.broadcasted_iota(jnp.int32, below_ref.shape, 1)
    edge_ref[...] = jnp.where(lane % EDGE < 2, below_ref[...], above_ref[...])
    return edge_ref


def small_steps(local, ex, ey, ez, hx, hy, hz, ey_x, ez_x):
    shifts = local.shifts
    every = range(len(ex))
    ez_y, ex_y = shifts.y_up(ez), shifts.y_up(ex)
    new_x = None
    if hx is not None:
        new_x = [hx[t] - COURANT * (ez_y[t] - ez[t] - (shifts.z_up(ey[t]) - ey[t])) for t in every]
    diff_z = [-ez[t] if ez_x is None else ez_x[t] - ez[t] for t in every]
    diff_y = [-ey[t] if ey_x is None else ey_x[t] - ey[t] for t in every]
    new_y = [hy[t] - COURANT * (shifts.z_up(ex[t]) - ex[t] - diff_z[t]) for t in every]
    new_z = [hz[t] - COURANT * (diff_y[t] - (ex_y[t] - ex[t])) for t in every]
    return new_x, new_y, new_z


def grown(local, ex, ey, ez, hx, hy, hz, hy_x, hz_x, half, source, count):
    shifts = local.shifts
    hz_y, hx_y = shifts.y_down(hz), shifts.y_down(hx)
    new_x, new_y, new_z = [], [], []
    for t in range(count):
        diff_y = hz[t] if hz_x is None else hz[t] - hz_x[t]
        diff_z = hy[t] if hy_x is None else hy[t] - hy_x[t]
        if ex is not None:
            new_x.append(ex[t] + half[t] * (hz[t] - hz_y[t] - (hy[t] - shifts.z_down(hy[t]))))
        new_y.append(ey[t] + half[t] * (hx[t] - shifts.z_down(hx[t]) - diff_y))
        new_z.append(ez[t] + half[t] * (diff_z - (hx[t] - hx_y[t])) + source[t])
    return new_x, new_y, new_z


def started(dims, two, field_ref, below_ref, above_ref, small_ref, half_ref, mask_ref, edge_ref):
    edges = merged_edges(below_ref, None if two else above_ref, edge_ref)
    return Local(dims, field_ref, edges, small_ref, half_ref, mask_ref)


def store_tiles(ref, unit, values, tiles, nz):
    for t in range(tiles):
        at = (unit * tiles + t) * nz
        ref[at:at + nz, :] = values[t]


def lower_kernel(dims, two, *refs):
    nz, _, tiles = dims
    *given, material_ref, down_ref, edge_ref = refs
    local = started(dims, two, *given, edge_ref)
    local.material = [material_ref[local.rows(0, t), :].astype(jnp.float32) for t in range(tiles)]
    half = local.half(0)
    edges = [None] * 17
    for run in range(2):
        low = [local.load(run, comp, 0) for comp in range(6)]
        nearer = [local.load(run, comp, 1) for comp in (1, 2)]
        source = local.source(run, 0, 0)
        for part in range(2):
            ex, ey, ez, hx, hy, hz = [low[comp][part] for comp in range(6)]
            hx, hy, hz = small_steps(local, ex, ey, ez, hx, hy, hz, nearer[0][part], nearer[1][part])
            _, new_y, new_z = grown(local, None, ey, ez, hx, hy, hz, None, None, half, source[part], tiles + 1)
            for which, value, initial in ((0, new_y, ey), (1, new_z, ez)):
                unit = (run * 2 + part) * 2 + which
                store_tiles(down_ref, unit, value, tiles, nz)
                edges[unit] = initial[tiles]
                edges[8 + unit] = value[tiles]
    edges[16] = unpack_edge(local.edge(0), 24)
    store_tiles(down_ref, 8, local.material, tiles, nz)
    at = 9 * tiles * nz
    down_ref[at:at + nz, :] = pack_edges(edges, local.shifts.lane)


def upper_kernel(dims, two, *refs):
    nz, width_x, tiles = dims
    *given, _, up_ref, edge_ref = refs
    local = started(dims, two, *given, edge_ref)
    edges = []
    for run in range(2):
        high = [local.load(run, comp, width_x - 1) for comp in (0, 1, 2, 4, 5)]
        for part in range(2):
            ex, ey, ez, hy, hz = [values[part] for values in high]
            _, hy, hz = small_steps(local, ex, ey, ez, None, hy, hz, None, None)
            for which, value in ((0, hy), (1, hz)):
                store_tiles(up_ref, (run * 2 + part) * 2 + which, value, tiles, nz)
                edges.append(value[tiles])
    at = 8 * tiles * nz
    up_ref[at:at + nz, :] = pack_edges(edges, local.shifts.lane)


def halo(local, ref, edge, first_spot, run, which, row):
    nz, tiles = local.nz, local.tiles
    units = [(run * 2 + part) * 2 + which for part in range(2)]
    values = [
        [ref[(unit * tiles + t) * nz:(unit * tiles + t + 1) * nz, :] for t in range(tiles)]
        + [unpack_edge(edge, first_spot + unit)]
        for unit in units
    ]
    turned = [turn(values[0][t], values[1][t], *local.angle(row, run)) for t in range(tiles + 1)]
    return [[value[part] for value in turned] for part in range(2)]


def half_above(local, down_ref, edge):
    nz, tiles = local.nz, local.tiles
    own = [down_ref[(8 * tiles + t) * nz:(8 * tiles + t + 1) * nz, :] for t in range(tiles)]
    levels = local.levels()
    return [COURANT * inverse_eps(value, levels) for value in own + [unpack_edge(edge, 16)]]


def share_kernel(dims, two, *refs):
    nz, width_x, tiles = dims
    *given, face_ref, down_ref, share_ref, edge_ref = refs
    local = started(dims, two, *given, edge_ref)
    edge = down_ref[9 * tiles * nz:(9 * tiles + 1) * nz, :]
    half = local.half(width_x - 1)
    above = half_above(local, down_ref, edge)
    kept_e, kept_h = {}, {}
    every = range(tiles + 1)
    for run in range(2):
        low = [local.load(run, comp, width_x - 2) for comp in range(6)]
        high = [local.load(run, comp, width_x - 1) for comp in range(6)]
        source = local.source(run, 0, width_x - 1)
        early = [halo(local, face_ref, edge, 0, run, which, AHEAD) for which in range(2)]
        later = [halo(local, down_ref, edge, 8, run, which, AHEAD) for which in range(2)]
        for part in range(2):
            ex, ey, ez, hx, hy, hz = [high[comp][part] for comp in range(6)]
            low_x, low_y, low_z, _, low_hy, low_hz = [low[comp][part] for comp in range(6)]
            _, low_hy, low_hz = small_steps(local, low_x, low_y, low_z, None, low_hy, low_hz, ey, ez)
            hx, hy, hz = small_steps(local, ex, ey, ez, hx, hy, hz, early[0][part], early[1][part])
            ex, ey, ez = grown(local, ex, ey, ez, hx, hy, hz, low_hy, low_hz, half, source[part], tiles + 1)
            above_y = [later[0][part][t] + above[t] * hz[t] for t in every]
            above_z = [later[1][part][t] - above[t] * hy[t] for t in every]
            _, hy, hz = small_steps(local, ex, ey, ez, None, hy, hz, above_y, above_z)
            kept_e[run, part] = (above_y, above_z)
            kept_h[run, part] = (hy, hz)
    for t in range(tiles):
        total = 0.0
        for run in range(2):
            for which, sign in ((0, 1.0), (1, -1.0)):
                term = (
                    kept_e[run, 0][which][t] * kept_h[1 - run, 0][1 - which][t]
                    - kept_e[run, 1][which][t] * kept_h[1 - run, 1][1 - which][t]
                )
                total = total + sign * term
        share_ref[t * nz:(t + 1) * nz, :] = above[t] * total


def product(now, later, t):
    return now[0, 0][t] * later[1, 0][t] - now[0, 1][t] * later[1, 1][t]


def both(one, two, t):
    return product(one, two, t) + product(two, one, t)


def interior_kernel(dims, two, *refs):
    nz, width_x, tiles = dims
    *given, face_ref, down_ref, kept_ref, cross_ref, edge_ref = refs
    local = started(dims, two, *given, edge_ref)
    every, own, layers = range(tiles + 1), range(tiles), range(width_x)
    edge = down_ref[9 * tiles * nz:(9 * tiles + 1) * nz, :]
    half = [local.half(x) for x in layers]
    above = half_above(local, down_ref, edge)
    kept_one, kept_two = {}, {}
    for run in range(2):
        sources = [[local.source(run, step, x) for x in layers] for step in range(2)]
        fields = [[local.load(run, comp, x) for x in layers] for comp in range(6)]
        early = [halo(local, face_ref, edge, 0, run, which, AHEAD) for which in range(2)]
        later = [halo(local, down_ref, edge, 8, run, which, AHEAD) for which in range(2)]
        for part in range(2):
            ex, ey, ez, hx, hy, hz = [[fields[comp][x][part] for x in layers] for comp in range(6)]
            under_y = [COURANT * ez[0][t] for t in every]
            under_z = [-COURANT * ey[0][t] for t in every]
            above_y, above_z = early[0][part], early[1][part]
            for step in range(2):
                ey_x, ez_x = ey[1:] + [above_y], ez[1:] + [above_z]
                for x in layers:
                    hx[x], hy[x], hz[x] = small_steps(
                        local, ex[x], ey[x], ez[x], hx[x], hy[x], hz[x], ey_x[x], ez_x[x]
                    )
                if step == 0:
                    above_y = [later[0][part][t] + above[t] * hz[-1][t] for t in every]
                    above_z = [later[1][part][t] - above[t] * hy[-1][t] for t in every]
                else:
                    under_y, under_z = None, None
                for x in layers:
                    hy_x, hz_x = (under_y, under_z) if x == 0 else (hy[x - 1], hz[x - 1])
                    ex[x], ey[x], ez[x] = grown(
                        local, ex[x], ey[x], ez[x], hx[x], hy[x], hz[x], hy_x, hz_x, half[x], sources[step][x][part],
                        tiles if step else tiles + 1,
                    )
                for x in layers:
                    for comp, value in enumerate((ex[x], ey[x], ez[x])):
                        (kept_two if step else kept_one).setdefault((comp, x), {})[run, part] = value
    for pair in range(4):
        where = (pair // 2, pair % 2)
        for comp in range(3):
            store_tiles(kept_ref, pair * 8 + comp, kept_one[comp, 0][where], tiles, nz)
            store_tiles(kept_ref, pair * 8 + 3 + comp, kept_two[comp, 0][where], tiles, nz)
        for comp in (1, 2):
            store_tiles(kept_ref, pair * 8 + 5 + comp, kept_one[comp, 1][where], tiles, nz)
    store_tiles(kept_ref, 32, half[0], tiles, nz)
    at = 33 * tiles * nz
    kept_ref[at:at + nz, :] = half[0][tiles]
    for x in range(1, width_x):
        for t in own:
            total = 0.0
            for comp in range(3):
                total = total + both(kept_one[comp, x], kept_two[comp, x], t)
            cross_ref[local.rows(x, t), :] = -half[x][t] * total
    for t in own:
        cross_ref[local.rows(0, t), :] = half[0][t]


def final_kernel(dims, small_ref, half_ref, kept_ref, inner_ref, up_ref, share_ref, cross_ref):
    nz, width_x, tiles = dims
    local = Local(dims, None, None, small_ref, half_ref, None)
    shifts = local.shifts
    every, own = range(tiles + 1), range(tiles)

    def tile(ref, unit, t):
        return ref[(unit * tiles + t) * nz:(unit * tiles + t + 1) * nz, :]

    half = [tile(kept_ref, 32, t) for t in every]
    next_half = [tile(half_ref, 1, t) for t in own]
    edge = up_ref[8 * tiles * nz:(8 * tiles + 1) * nz, :]
    one, two, next_one, next_add = [[{} for _ in range(3)] for _ in range(4)]
    for run in range(2):
        under = [halo(local, up_ref, edge, 0, run, which, BACK) for which in range(2)]
        for part in range(2):
            pair = run * 2 + part
            add_y = [half[t] * under[1][part][t] for t in every]
            add_z = [-half[t] * under[0][part][t] for t in every]
            add_z_y = shifts.y_up(add_z)
            hx = [-COURANT * (add_z_y[t] - add_z[t] - (shifts.z_up(add_y[t]) - add_y[t])) for t in every]
            hy = [-COURANT * add_z[t] for t in every]
            hz = [COURANT * add_y[t] for t in every]
            hz_y, hx_y = shifts.y_down(hz), shifts.y_down(hx)
            more = [
                [half[t] * (hz[t] - hz_y[t] - (hy[t] - shifts.z_down(hy[t]))) for t in own],
                [add_y[t] + half[t] * (hx[t] - shifts.z_down(hx[t]) - hz[t]) for t in own],
                [add_z[t] + half[t] * (hy[t] - (hx[t] - hx_y[t])) for t in own],
            ]
            first = [None, add_y, add_z]
            for comp in range(3):
                value = [tile(kept_ref, pair * 8 + comp, t) for t in own]
                one[comp][run, part] = value if comp == 0 else [value[t] + first[comp][t] for t in own]
                two[comp][run, part] = [tile(kept_ref, pair * 8 + 3 + comp, t) + more[comp][t] for t in own]
            for comp, value in ((1, hz), (2, [-hy[t] for t in own])):
                next_one[comp][run, part] = [tile(kept_ref, pair * 8 + 5 + comp, t) for t in own]
                next_add[comp][run, part] = [next_half[t] * value[t] for t in own]
    for t in own:
        total = share_ref[t * nz:(t + 1) * nz, :]
        for comp in range(3):
            total = total + both(one[comp], two[comp], t)
        cross_ref[local.rows(0, t), :] = -half[t] * total
        total = both(next_one[1], next_add[1], t) + both(next_one[2], next_add[2], t)
        cross_ref[local.rows(1, t), :] = inner_ref[local.rows(1, t), :] - next_half[t] * total
        for x in range(2, width_x):
            cross_ref[local.rows(x, t), :] = inner_ref[local.rows(x, t), :]


def sum_kernel(own_ref, other_ref, out_ref):
    out_ref[...] = own_ref[...] + other_ref[...]


VMEM = pl.BlockSpec(memory_space=pltpu.VMEM)
SMEM = pl.BlockSpec(memory_space=pltpu.SMEM)


HBM = pl.BlockSpec(memory_space=pltpu.HBM)
MIB = 1024 * 1024


def call(kernel, name, in_specs, rows, cost, scratch=(), limit=48 * MIB):
    shapes = [jax.ShapeDtypeStruct((count, LANES), jnp.float32) for count in rows]
    return pl.pallas_call(
        kernel,
        name=name,
        out_shape=shapes,
        in_specs=in_specs,
        out_specs=[VMEM] * len(shapes),
        scratch_shapes=list(scratch),
        compiler_params=pltpu.CompilerParams(vmem_limit_bytes=limit),
        cost_estimate=pl.CostEstimate(flops=0, bytes_accessed=cost, transcendentals=0),
    )


def moved(value, axis, steps):
    count = lax.axis_size(axis)
    return lax.ppermute(value, axis, [(source, (source + steps) % count) for source in range(count)])


def local(field_state, material_map, eps_table, bloch_phase, source_cells, source_wave):
    nz, width_x, width_y = material_map.shape
    tiles = width_y // LANES
    dims = (nz, width_x, tiles)
    rows = nz * tiles * width_x
    fields = field_state.reshape(24, nz, width_x, tiles, LANES).transpose(0, 1, 3, 2, 4).reshape(24, rows, LANES)
    material = material_map.reshape(nz, width_x, tiles, LANES).transpose(0, 2, 1, 3).reshape(rows, LANES)
    unit = nz * tiles
    two = lax.axis_size("gy") == 2
    levels = eps_table.shape[0]

    (face,) = call(
        functools.partial(face_kernel, dims), "faces", [HBM], [8 * unit], 100_000,
        (pltpu.VMEM((4, 2, rows, LANES), jnp.float32), pltpu.SemaphoreType.DMA((4,))),
        53 * MIB,
    )(fields)
    (edge,) = call(functools.partial(edge_kernel, dims), "edges", [VMEM] * 3, [width_x * nz], 80_000_000)(
        face, fields, material
    )
    small, half, mask = call(
        functools.partial(prepare_kernel, dims), "prepare", [VMEM] * 2 + [SMEM] * 4,
        [LEVELS + levels, rows, 2 * width_x * (tiles + 1) * nz], 20_000_000,
    )(edge, material, eps_table, bloch_phase, source_cells, source_wave)
    face = moved(face, "gx", -1)
    below = moved(edge, "gy", 1)
    above = below if two else moved(edge, "gy", -1)
    given = (fields, below, above, small, half, mask)
    specs = [VMEM] * len(given)
    scratch = (pltpu.VMEM((width_x * nz, LANES), jnp.float32),)

    def stage(kernel, name, cost, rows, *more):
        return call(
            functools.partial(kernel, dims, two), name, specs + [VMEM] * len(more), rows, cost, scratch
        )(*given, *more)

    down = moved(stage(lower_kernel, "lower", 20_000_000, [9 * unit + nz], material)[0], "gx", -1)
    up = moved(stage(upper_kernel, "upper", 20_000_000, [8 * unit + nz], face)[0], "gx", 1)
    share = moved(stage(share_kernel, "share", 20_000_000, [unit], face, down)[0], "gx", 1)
    kept, inner = stage(interior_kernel, "interior", 20_000_000, [33 * unit + nz, rows], face, down)
    (cross,) = call(functools.partial(final_kernel, dims), "final", [VMEM] * 6, [rows], 2_000_000)(
        small, half, kept, inner, up, share
    )
    other = moved(cross, "src", 1)
    (out,) = call(sum_kernel, "gradient", [VMEM, VMEM], [rows], 500_000)(cross, other)
    return out.reshape(nz, tiles, width_x, LANES).transpose(0, 2, 1, 3).reshape(nz, width_x, width_y)


def solution(mesh):
    return jax.shard_map(
        local,
        mesh=mesh,
        in_specs=(
            P(("design", "src"), None, None, None, None, "gx", "gy"),
            P("design", "gx", "gy"),
            P(),
            P("design"),
            P(("design", "src"), None),
            P(("design", "src"), None, None, None),
        ),
        out_specs=P("design", "gx", "gy"),
        check_vma=False,
    )
```

```python
import functools

import jax
import jax.numpy as jnp
from jax import lax
from jax.experimental import pallas as pl
from jax.experimental.pallas import tpu as pltpu
from jax.sharding import PartitionSpec as P

COURANT = 0.5
LANES = 128
MATERIAL_MOVE = 95
EDGE = 4


def lane_iota(nz):
    return lax.broadcasted_iota(jnp.int32, (nz, LANES), 1)


def row_iota(nz):
    return lax.broadcasted_iota(jnp.int32, (nz, LANES), 0)


def pack_edges(values, lane):
    packed = jnp.zeros_like(values[0])
    for spot, value in enumerate(values):
        moved = pltpu.roll(value, EDGE * spot + 2, 1)
        packed = jnp.where(lane // EDGE == spot, moved, packed)
    return packed


def unpack_edge(packed, spot):
    return pltpu.roll(packed, LANES - EDGE * spot - 2, 1)


def folded(packed, width):
    groups = LANES // width
    rows = packed.shape[0] // groups
    lane = lax.broadcasted_iota(jnp.int32, (rows, LANES), 1)
    result = packed[0:rows]
    for group in range(1, groups):
        moved = pltpu.roll(packed[group * rows:(group + 1) * rows], group * width, 1)
        result = jnp.where(lane // width == group, moved, result)
    return result


def unfolded(values, width):
    groups = LANES // width
    return jnp.concatenate(
        [values] + [pltpu.roll(values, LANES - group * width, 1) for group in range(1, groups)], axis=0
    )


class Shifts:
    def __init__(self, nz):
        self.nz = nz
        self.row = row_iota(nz)
        self.lane = lane_iota(nz)

    def z_up(self, value):
        return jnp.where(self.row == self.nz - 1, 0.0, pltpu.roll(value, self.nz - 1, 0))

    def z_down(self, value):
        return jnp.where(self.row == 0, 0.0, pltpu.roll(value, 1, 0))

    def y_up(self, tiles):
        moved = [pltpu.roll(value, LANES - 1, 1) for value in tiles]
        count = len(tiles)
        return [jnp.where(self.lane == LANES - 1, moved[(t + 1) % count], moved[t]) for t in range(count)]

    def y_down(self, tiles):
        moved = [pltpu.roll(value, 1, 1) for value in tiles]
        count = len(tiles)
        return [jnp.where(self.lane == 0, moved[(t - 1) % count], moved[t]) for t in range(count)]


def turn(real_part, imag_part, cosine, sine):
    return real_part * cosine - imag_part * sine, real_part * sine + imag_part * cosine


def inverse_eps(material, levels):
    level = levels[0]
    for index in range(1, len(levels)):
        level = jnp.where(material == index, levels[index], level)
    return 1.0 / level


AHEAD, BACK, EDGES, WAVE, TURNED, LEVELS = 0, 2, 4, 8, 16, 24


def spot_of(run, part, comp):
    return (run * 2 + part) * 6 + comp


class Local:
    def __init__(self, dims, field_ref, edge_ref, small_ref, half_ref, mask_ref):
        self.nz, self.width_x, self.tiles = dims
        self.field_ref, self.edge_ref = field_ref, edge_ref
        self.small_ref, self.half_ref, self.mask_ref = small_ref, half_ref, mask_ref
        self.shifts = Shifts(self.nz)

    def rows(self, x, t):
        return pl.ds(t * self.width_x + x, self.nz, stride=self.tiles * self.width_x)

    def own(self, run, part, comp, x, t):
        return self.field_ref[spot_of(run, part, comp), self.rows(x, t), :]

    def edge(self, x):
        return self.edge_ref[x * self.nz:(x + 1) * self.nz, :]

    def small(self, row):
        return self.small_ref[row:row + 1, :]

    def angle(self, row, run):
        sine = self.small(row + 1)
        return self.small(row), sine if run == 0 else -sine

    def levels(self):
        return [self.small(row) for row in range(LEVELS, self.small_ref.shape[0])]

    def load(self, run, comp, x):
        packed = self.edge(x)
        parts = [[self.own(run, part, comp, x, t) for t in range(self.tiles)] for part in range(2)]
        edges = [unpack_edge(packed, spot_of(run, part, comp)) for part in range(2)]
        edges = turn(edges[0], edges[1], *self.angle(EDGES, run))
        return [parts[part] + [edges[part]] for part in range(2)]

    def half(self, x):
        starts = [(x * self.tiles + t) * self.nz for t in range(self.tiles)]
        own = [self.half_ref[at:at + self.nz, :] for at in starts]
        return own + [COURANT * inverse_eps(unpack_edge(self.edge(x), 24), self.levels())]

    def source(self, run, step, x):
        parts = []
        for part in range(2):
            values = []
            for t in range(self.tiles + 1):
                at = ((run * self.width_x + x) * (self.tiles + 1) + t) * self.nz
                row = (WAVE if t < self.tiles else TURNED) + (run * 2 + part) * 2 + step
                values.append(self.mask_ref[at:at + self.nz, :] * self.small(row))
            parts.append(values)
        return parts


def face_kernel(dims, field_hbm, face_ref, planes_ref, sems):
    nz, width_x, tiles = dims
    copies = [
        pltpu.make_async_copy(field_hbm.at[pl.ds(6 * pair + 1, 2)], planes_ref.at[pair], sems.at[pair])
        for pair in range(4)
    ]
    for copy in copies:
        copy.start()
    for pair in range(4):
        copies[pair].wait()
        for which in range(2):
            values = [planes_ref[pair, which, pl.ds(t * width_x, nz, stride=tiles * width_x), :] for t in range(tiles)]
            store_tiles(face_ref, pair * 2 + which, values, tiles, nz)


def edge_kernel(dims, order_ref, field_ref, material_ref, edge_ref):
    nz, width_x, tiles = dims
    local = Local(dims, field_ref, None, None, None, None)
    lane = lane_iota(nz)
    for x in range(width_x):
        values = []
        for run in range(2):
            for part in range(2):
                for comp in range(6):
                    values.append(
                        jnp.where(
                            lane < LANES // 2,
                            local.own(run, part, comp, x, 0),
                            local.own(run, part, comp, x, tiles - 1),
                        )
                    )
        material = jnp.where(
            lane < LANES // 2, material_ref[local.rows(x, 0), :], material_ref[local.rows(x, tiles - 1), :]
        )
        values.append(material.astype(jnp.float32))
        edge_ref[x * nz:(x + 1) * nz, :] = pack_edges(values, lane)


def prepare_kernel(
    dims, order_ref, material_ref, table_ref, phase_ref, cells_ref, wave_ref, small_ref, half_ref, mask_ref,
):
    nz, width_x, tiles = dims
    row = lax.broadcasted_iota(jnp.int32, (8, LANES), 0)
    angle = jnp.where(row == 0, phase_ref[0], phase_ref[1])
    cosine, sine = jnp.cos(angle), jnp.sin(angle)
    cosine_x, sine_x, cosine_y, sine_y = cosine[0:1], sine[0:1], cosine[1:2], sine[1:2]
    first_x, first_y = lax.axis_index("gx") == 0, lax.axis_index("gy") == 0
    last_x = lax.axis_index("gx") == lax.axis_size("gx") - 1
    last_y = lax.axis_index("gy") == lax.axis_size("gy") - 1
    small_ref[AHEAD:AHEAD + 1, :] = jnp.where(last_x, cosine_x, 1.0)
    small_ref[AHEAD + 1:AHEAD + 2, :] = jnp.where(last_x, sine_x, 0.0)
    small_ref[BACK:BACK + 1, :] = jnp.where(first_x, cosine_x, 1.0)
    small_ref[BACK + 1:BACK + 2, :] = jnp.where(first_x, -sine_x, 0.0)
    upper = lax.broadcasted_iota(jnp.int32, (1, LANES), 1) < LANES // 2
    cosine = jnp.where(upper, jnp.where(last_y, cosine_y, 1.0), jnp.where(first_y, cosine_y, 1.0))
    sine = jnp.where(upper, jnp.where(last_y, sine_y, 0.0), jnp.where(first_y, -sine_y, 0.0))
    small_ref[EDGES:EDGES + 1, :] = cosine
    small_ref[EDGES + 1:EDGES + 2, :] = sine
    small_ref[EDGES + 2:WAVE, :] = jnp.zeros((WAVE - EDGES - 2, LANES), jnp.float32)
    for run in range(2):
        for step in range(2):
            spots = [(run * 2 + part) * 2 + step for part in range(2)]
            amplitude = [wave_ref[0, run, part, step] for part in range(2)]
            turned = turn(amplitude[0], amplitude[1], cosine, sine if run == 0 else -sine)
            for part in range(2):
                row = WAVE + spots[part]
                small_ref[row:row + 1, :] = jnp.full((1, LANES), amplitude[part], jnp.float32)
                row = TURNED + spots[part]
                small_ref[row:row + 1, :] = turned[part]
    for index in range(table_ref.shape[0]):
        small_ref[LEVELS + index:LEVELS + index + 1, :] = jnp.full((1, LANES), table_ref[index], jnp.float32)
    levels = [table_ref[index] for index in range(table_ref.shape[0])]
    total_x = width_x * lax.axis_size("gx")
    width_y = tiles * LANES
    total_y = width_y * lax.axis_size("gy")
    begin_y = lax.axis_index("gy") * width_y
    z, lane = row_iota(nz), lane_iota(nz)
    for x in range(width_x):
        plane = z * total_x + lax.axis_index("gx") * width_x + x
        for t in range(tiles + 1):
            if t < tiles:
                column = begin_y + t * LANES + lane
                material = material_ref[pl.ds(t * width_x + x, nz, stride=tiles * width_x), :]
                at = (x * tiles + t) * nz
                half_ref[at:at + nz, :] = COURANT * inverse_eps(material, levels)
            else:
                column = begin_y + jnp.where(lane < LANES // 2, lane + width_y, lane - LANES)
                column = jnp.where(column < 0, column + total_y, column)
                column = jnp.where(column >= total_y, column - total_y, column)
            index = plane * total_y + column
            for run in range(2):
                at = ((run * width_x + x) * (tiles + 1) + t) * nz
                mask_ref[at:at + nz, :] = jnp.where(index == cells_ref[0, run], 1.0, 0.0)


def merged_edges(below_ref, above_ref, edge_ref):
    if above_ref is None:
        return below_ref
    lane = lax.broadcasted_iota(jnp.int32, below_ref.shape, 1)
    edge_ref[...] = jnp.where(lane % EDGE < 2, below_ref[...], above_ref[...])
    return edge_ref


def small_steps(local, ex, ey, ez, hx, hy, hz, ey_x, ez_x):
    shifts = local.shifts
    every = range(len(ex))
    ez_y, ex_y = shifts.y_up(ez), shifts.y_up(ex)
    new_x = None
    if hx is not None:
        new_x = [hx[t] - COURANT * (ez_y[t] - ez[t] - (shifts.z_up(ey[t]) - ey[t])) for t in every]
    diff_z = [-ez[t] if ez_x is None else ez_x[t] - ez[t] for t in every]
    diff_y = [-ey[t] if ey_x is None else ey_x[t] - ey[t] for t in every]
    new_y = [hy[t] - COURANT * (shifts.z_up(ex[t]) - ex[t] - diff_z[t]) for t in every]
    new_z = [hz[t] - COURANT * (diff_y[t] - (ex_y[t] - ex[t])) for t in every]
    return new_x, new_y, new_z


def grown(local, ex, ey, ez, hx, hy, hz, hy_x, hz_x, half, source, count):
    shifts = local.shifts
    hz_y, hx_y = shifts.y_down(hz), shifts.y_down(hx)
    new_x, new_y, new_z = [], [], []
    for t in range(count):
        diff_y = hz[t] if hz_x is None else hz[t] - hz_x[t]
        diff_z = hy[t] if hy_x is None else hy[t] - hy_x[t]
        if ex is not None:
            new_x.append(ex[t] + half[t] * (hz[t] - hz_y[t] - (hy[t] - shifts.z_down(hy[t]))))
        new_y.append(ey[t] + half[t] * (hx[t] - shifts.z_down(hx[t]) - diff_y))
        new_z.append(ez[t] + half[t] * (diff_z - (hx[t] - hx_y[t])) + source[t])
    return new_x, new_y, new_z


def started(dims, two, field_ref, below_ref, above_ref, small_ref, half_ref, mask_ref, edge_ref):
    edges = merged_edges(below_ref, None if two else above_ref, edge_ref)
    return Local(dims, field_ref, edges, small_ref, half_ref, mask_ref)


def store_tiles(ref, unit, values, tiles, nz):
    for t in range(tiles):
        at = (unit * tiles + t) * nz
        ref[at:at + nz, :] = values[t]


def lower_kernel(dims, two, *refs):
    nz, _, tiles = dims
    *given, material_ref, down_ref, edge_ref = refs
    local = started(dims, two, *given, edge_ref)
    local.material = [material_ref[local.rows(0, t), :].astype(jnp.float32) for t in range(tiles)]
    half = local.half(0)
    edges = [None] * 16
    for run in range(2):
        low = [local.load(run, comp, 0) for comp in range(6)]
        nearer = [local.load(run, comp, 1) for comp in (1, 2)]
        source = local.source(run, 0, 0)
        for part in range(2):
            ex, ey, ez, hx, hy, hz = [low[comp][part] for comp in range(6)]
            hx, hy, hz = small_steps(local, ex, ey, ez, hx, hy, hz, nearer[0][part], nearer[1][part])
            _, new_y, new_z = grown(local, None, ey, ez, hx, hy, hz, None, None, half, source[part], tiles + 1)
            for which, value, initial in ((0, new_y, ey), (1, new_z, ez)):
                unit = (run * 2 + part) * 2 + which
                store_tiles(down_ref, unit, value, tiles, nz)
                edges[unit] = initial[tiles]
                edges[8 + unit] = value[tiles]
    store_tiles(down_ref, 8, local.material, tiles, nz)
    packed = pack_edges(edges, local.shifts.lane)
    column = pltpu.roll(unpack_edge(local.edge(0), 24), LANES - MATERIAL_MOVE, 1)
    packed = jnp.where(local.shifts.lane == EDGE * 8, column, packed)
    down_ref[9 * tiles * nz:, :] = folded(packed, 64)


def upper_kernel(dims, two, *refs):
    nz, width_x, tiles = dims
    *given, _, up_ref, edge_ref = refs
    local = started(dims, two, *given, edge_ref)
    edges = []
    for run in range(2):
        high = [local.load(run, comp, width_x - 1) for comp in (0, 1, 2, 4, 5)]
        for part in range(2):
            ex, ey, ez, hy, hz = [values[part] for values in high]
            _, hy, hz = small_steps(local, ex, ey, ez, None, hy, hz, None, None)
            for which, value in ((0, hy), (1, hz)):
                store_tiles(up_ref, (run * 2 + part) * 2 + which, value, tiles, nz)
                edges.append(value[tiles])
    up_ref[8 * tiles * nz:, :] = folded(pack_edges(edges, local.shifts.lane), 32)


def halo(local, ref, edge, first_spot, run, which, row):
    nz, tiles = local.nz, local.tiles
    units = [(run * 2 + part) * 2 + which for part in range(2)]
    values = [
        [ref[(unit * tiles + t) * nz:(unit * tiles + t + 1) * nz, :] for t in range(tiles)]
        + [unpack_edge(edge, first_spot + unit)]
        for unit in units
    ]
    turned = [turn(values[0][t], values[1][t], *local.angle(row, run)) for t in range(tiles + 1)]
    return [[value[part] for value in turned] for part in range(2)]


def half_above(local, down_ref, edge):
    nz, tiles = local.nz, local.tiles
    own = [down_ref[(8 * tiles + t) * nz:(8 * tiles + t + 1) * nz, :] for t in range(tiles)]
    levels = local.levels()
    return [COURANT * inverse_eps(value, levels) for value in own + [pltpu.roll(edge, MATERIAL_MOVE, 1)]]


def share_kernel(dims, two, *refs):
    nz, width_x, tiles = dims
    *given, face_ref, down_ref, share_ref, edge_ref = refs
    local = started(dims, two, *given, edge_ref)
    edge = unfolded(down_ref[9 * tiles * nz:, :], 64)
    half = local.half(width_x - 1)
    above = half_above(local, down_ref, edge)
    kept_e, kept_h = {}, {}
    every = range(tiles + 1)
    for run in range(2):
        low = [local.load(run, comp, width_x - 2) for comp in range(6)]
        high = [local.load(run, comp, width_x - 1) for comp in range(6)]
        source = local.source(run, 0, width_x - 1)
        early = [halo(local, face_ref, edge, 0, run, which, AHEAD) for which in range(2)]
        later = [halo(local, down_ref, edge, 8, run, which, AHEAD) for which in range(2)]
        for part in range(2):
            ex, ey, ez, hx, hy, hz = [high[comp][part] for comp in range(6)]
            low_x, low_y, low_z, _, low_hy, low_hz = [low[comp][part] for comp in range(6)]
            _, low_hy, low_hz = small_steps(local, low_x, low_y, low_z, None, low_hy, low_hz, ey, ez)
            hx, hy, hz = small_steps(local, ex, ey, ez, hx, hy, hz, early[0][part], early[1][part])
            ex, ey, ez = grown(local, ex, ey, ez, hx, hy, hz, low_hy, low_hz, half, source[part], tiles + 1)
            above_y = [later[0][part][t] + above[t] * hz[t] for t in every]
            above_z = [later[1][part][t] - above[t] * hy[t] for t in every]
            _, hy, hz = small_steps(local, ex, ey, ez, None, hy, hz, above_y, above_z)
            kept_e[run, part] = (above_y, above_z)
            kept_h[run, part] = (hy, hz)
    for t in range(tiles):
        total = 0.0
        for run in range(2):
            for which, sign in ((0, 1.0), (1, -1.0)):
                term = (
                    kept_e[run, 0][which][t] * kept_h[1 - run, 0][1 - which][t]
                    - kept_e[run, 1][which][t] * kept_h[1 - run, 1][1 - which][t]
                )
                total = total + sign * term
        share_ref[t * nz:(t + 1) * nz, :] = above[t] * total


def product(now, later, t):
    return now[0, 0][t] * later[1, 0][t] - now[0, 1][t] * later[1, 1][t]


def both(one, two, t):
    return product(one, two, t) + product(two, one, t)


def interior_kernel(dims, two, *refs):
    nz, width_x, tiles = dims
    *given, face_ref, down_ref, _, kept_ref, cross_ref, edge_ref = refs
    local = started(dims, two, *given, edge_ref)
    every, own, layers = range(tiles + 1), range(tiles), range(width_x)
    edge = unfolded(down_ref[9 * tiles * nz:, :], 64)
    half = [local.half(x) for x in layers]
    above = half_above(local, down_ref, edge)
    kept_one, kept_two = {}, {}
    for run in range(2):
        sources = [[local.source(run, step, x) for x in layers] for step in range(2)]
        fields = [[local.load(run, comp, x) for x in layers] for comp in range(6)]
        early = [halo(local, face_ref, edge, 0, run, which, AHEAD) for which in range(2)]
        later = [halo(local, down_ref, edge, 8, run, which, AHEAD) for which in range(2)]
        for part in range(2):
            ex, ey, ez, hx, hy, hz = [[fields[comp][x][part] for x in layers] for comp in range(6)]
            under_y = [COURANT * ez[0][t] for t in every]
            under_z = [-COURANT * ey[0][t] for t in every]
            above_y, above_z = early[0][part], early[1][part]
            for step in range(2):
                ey_x, ez_x = ey[1:] + [above_y], ez[1:] + [above_z]
                for x in layers:
                    hx[x], hy[x], hz[x] = small_steps(
                        local, ex[x], ey[x], ez[x], hx[x], hy[x], hz[x], ey_x[x], ez_x[x]
                    )
                if step == 0:
                    above_y = [later[0][part][t] + above[t] * hz[-1][t] for t in every]
                    above_z = [later[1][part][t] - above[t] * hy[-1][t] for t in every]
                else:
                    under_y, under_z = None, None
                for x in layers:
                    hy_x, hz_x = (under_y, under_z) if x == 0 else (hy[x - 1], hz[x - 1])
                    ex[x], ey[x], ez[x] = grown(
                        local, ex[x], ey[x], ez[x], hx[x], hy[x], hz[x], hy_x, hz_x, half[x], sources[step][x][part],
                        tiles if step else tiles + 1,
                    )
                for x in layers:
                    for comp, value in enumerate((ex[x], ey[x], ez[x])):
                        (kept_two if step else kept_one).setdefault((comp, x), {})[run, part] = value
    for pair in range(4):
        where = (pair // 2, pair % 2)
        for comp in range(3):
            store_tiles(kept_ref, pair * 8 + comp, kept_one[comp, 0][where], tiles, nz)
            store_tiles(kept_ref, pair * 8 + 3 + comp, kept_two[comp, 0][where], tiles, nz)
        for comp in (1, 2):
            store_tiles(kept_ref, pair * 8 + 5 + comp, kept_one[comp, 1][where], tiles, nz)
    store_tiles(kept_ref, 32, half[0], tiles, nz)
    at = 33 * tiles * nz
    kept_ref[at:at + nz, :] = half[0][tiles]
    for x in range(1, width_x):
        for t in own:
            total = 0.0
            for comp in range(3):
                total = total + both(kept_one[comp, x], kept_two[comp, x], t)
            cross_ref[local.rows(x, t), :] = -half[x][t] * total
    for t in own:
        cross_ref[local.rows(0, t), :] = half[0][t]


def final_kernel(dims, small_ref, half_ref, kept_ref, inner_ref, up_ref, *cross_refs):
    nz, width_x, tiles = dims
    local = Local(dims, None, None, small_ref, half_ref, None)
    shifts = local.shifts
    every, own = range(tiles + 1), range(tiles)

    def tile(ref, unit, t):
        return ref[(unit * tiles + t) * nz:(unit * tiles + t + 1) * nz, :]

    half = [tile(kept_ref, 32, t) for t in every]
    next_half = [tile(half_ref, 1, t) for t in own]
    edge = unfolded(up_ref[8 * tiles * nz:, :], 32)
    one, two, next_one, next_add = [[{} for _ in range(3)] for _ in range(4)]
    for run in range(2):
        under = [halo(local, up_ref, edge, 0, run, which, BACK) for which in range(2)]
        for part in range(2):
            pair = run * 2 + part
            add_y = [half[t] * under[1][part][t] for t in every]
            add_z = [-half[t] * under[0][part][t] for t in every]
            add_z_y = shifts.y_up(add_z)
            hx = [-COURANT * (add_z_y[t] - add_z[t] - (shifts.z_up(add_y[t]) - add_y[t])) for t in every]
            hy = [-COURANT * add_z[t] for t in every]
            hz = [COURANT * add_y[t] for t in every]
            hz_y, hx_y = shifts.y_down(hz), shifts.y_down(hx)
            more = [
                [half[t] * (hz[t] - hz_y[t] - (hy[t] - shifts.z_down(hy[t]))) for t in own],
                [add_y[t] + half[t] * (hx[t] - shifts.z_down(hx[t]) - hz[t]) for t in own],
                [add_z[t] + half[t] * (hy[t] - (hx[t] - hx_y[t])) for t in own],
            ]
            first = [None, add_y, add_z]
            for comp in range(3):
                value = [tile(kept_ref, pair * 8 + comp, t) for t in own]
                one[comp][run, part] = value if comp == 0 else [value[t] + first[comp][t] for t in own]
                two[comp][run, part] = [tile(kept_ref, pair * 8 + 3 + comp, t) + more[comp][t] for t in own]
            for comp, value in ((1, hz), (2, [-hy[t] for t in own])):
                next_one[comp][run, part] = [tile(kept_ref, pair * 8 + 5 + comp, t) for t in own]
                next_add[comp][run, part] = [next_half[t] * value[t] for t in own]
    for t in own:
        for x in range(width_x):
            if x == 0:
                total = 0.0
                for comp in range(3):
                    total = total + both(one[comp], two[comp], t)
                total = -half[t] * total
            else:
                total = inner_ref[local.rows(x, t), :]
                if x == 1:
                    total = total - next_half[t] * (
                        both(next_one[1], next_add[1], t) + both(next_one[2], next_add[2], t)
                    )
            cross_refs[x * tiles + t][...] = total


def sum_kernel(dims, half_ref, own_share_ref, other_share_ref, *refs):
    nz, width_x, tiles = dims
    *parts, out_ref = refs
    count = width_x * tiles
    for x in range(width_x):
        for t in range(tiles):
            index = x * tiles + t
            total = parts[index][...] + parts[count + index][...]
            if x == 0:
                span = slice(t * nz, (t + 1) * nz)
                total = total - half_ref[span, :] * (own_share_ref[span, :] + other_share_ref[span, :])
            out_ref[pl.ds(t * width_x + x, nz, stride=tiles * width_x), :] = total


VMEM = pl.BlockSpec(memory_space=pltpu.VMEM)
SMEM = pl.BlockSpec(memory_space=pltpu.SMEM)


HBM = pl.BlockSpec(memory_space=pltpu.HBM)
MIB = 1024 * 1024


def call(kernel, name, in_specs, rows, cost, scratch=(), limit=48 * MIB):
    shapes = [jax.ShapeDtypeStruct((count, LANES), jnp.float32) for count in rows]
    return pl.pallas_call(
        kernel,
        name=name,
        out_shape=shapes,
        in_specs=in_specs,
        out_specs=[VMEM] * len(shapes),
        scratch_shapes=list(scratch),
        compiler_params=pltpu.CompilerParams(vmem_limit_bytes=limit),
        cost_estimate=pl.CostEstimate(flops=0, bytes_accessed=cost, transcendentals=0),
    )


def moved(value, axis, steps):
    count = lax.axis_size(axis)
    return lax.ppermute(value, axis, [(source, (source + steps) % count) for source in range(count)])


def local(field_state, material_map, eps_table, bloch_phase, source_cells, source_wave):
    nz, width_x, width_y = material_map.shape
    tiles = width_y // LANES
    dims = (nz, width_x, tiles)
    rows = nz * tiles * width_x
    fields = field_state.reshape(24, nz, width_x, tiles, LANES).transpose(0, 1, 3, 2, 4).reshape(24, rows, LANES)
    material = material_map.reshape(nz, width_x, tiles, LANES).transpose(0, 2, 1, 3).reshape(rows, LANES)
    unit = nz * tiles
    two = lax.axis_size("gy") == 2
    levels = eps_table.shape[0]

    (face,) = call(
        functools.partial(face_kernel, dims), "faces", [HBM], [8 * unit], 100_000,
        (pltpu.VMEM((4, 2, rows, LANES), jnp.float32), pltpu.SemaphoreType.DMA((4,))),
        53 * MIB,
    )(fields)
    (edge,) = call(functools.partial(edge_kernel, dims), "edges", [VMEM] * 3, [width_x * nz], 80_000_000)(
        face, fields, material
    )
    small, half, mask = call(
        functools.partial(prepare_kernel, dims), "prepare", [VMEM] * 2 + [SMEM] * 4,
        [LEVELS + levels, rows, 2 * width_x * (tiles + 1) * nz], 20_000_000,
    )(edge, material, eps_table, bloch_phase, source_cells, source_wave)
    face = moved(face, "gx", -1)
    below = moved(edge, "gy", 1)
    above = below if two else moved(edge, "gy", -1)
    given = (fields, below, above, small, half, mask)
    specs = [VMEM] * len(given)
    scratch = (pltpu.VMEM((width_x * nz, LANES), jnp.float32),)

    def stage(kernel, name, cost, rows, *more):
        return call(
            functools.partial(kernel, dims, two), name, specs + [VMEM] * len(more), rows, cost, scratch
        )(*given, *more)

    down = moved(stage(lower_kernel, "lower", 20_000_000, [9 * unit + nz // 2], material)[0], "gx", -1)
    up = moved(stage(upper_kernel, "upper", 20_000_000, [8 * unit + nz // 4], face)[0], "gx", 1)
    (share,) = stage(share_kernel, "share", 20_000_000, [unit], face, down)
    count_x, count_src = lax.axis_size("gx"), lax.axis_size("src")
    own_share = moved(share, "gx", 1)
    other_share = lax.ppermute(
        share, ("gx", "src"),
        [
            (x * count_src + s, (x + 1) % count_x * count_src + (s + 1) % count_src)
            for x in range(count_x)
            for s in range(count_src)
        ],
    )
    kept, inner = stage(interior_kernel, "interior", 40_000_000, [33 * unit + nz, rows], face, down, share)
    cross = call(
        functools.partial(final_kernel, dims), "final", [VMEM] * 5, [nz] * (width_x * tiles), 1_000_000
    )(small, half, kept, inner, up)
    other = [moved(value, "src", 1) for value in cross]
    (out,) = call(
        functools.partial(sum_kernel, dims), "gradient", [VMEM] * (3 + 2 * len(other)), [rows], 10_000
    )(half, own_share, other_share, *cross, *other)
    return out.reshape(nz, tiles, width_x, LANES).transpose(0, 2, 1, 3).reshape(nz, width_x, width_y)


def solution(mesh):
    return jax.shard_map(
        local,
        mesh=mesh,
        in_specs=(
            P(("design", "src"), None, None, None, None, "gx", "gy"),
            P("design", "gx", "gy"),
            P(),
            P("design"),
            P(("design", "src"), None),
            P(("design", "src"), None, None, None),
        ),
        out_specs=P("design", "gx", "gy"),
        check_vma=False,
    )
```

```python
import functools

import jax
import jax.numpy as jnp
from jax import lax
from jax.experimental import pallas as pl
from jax.experimental.pallas import tpu as pltpu
from jax.sharding import PartitionSpec as P

COURANT = 0.5
LANES = 128
MATERIAL_MOVE = 95
EDGE = 4


def lane_iota(nz):
    return lax.broadcasted_iota(jnp.int32, (nz, LANES), 1)


def row_iota(nz):
    return lax.broadcasted_iota(jnp.int32, (nz, LANES), 0)


def pack_edges(values, lane):
    packed = jnp.zeros_like(values[0])
    for spot, value in enumerate(values):
        moved = pltpu.roll(value, EDGE * spot + 2, 1)
        packed = jnp.where(lane // EDGE == spot, moved, packed)
    return packed


def unpack_edge(packed, spot):
    return pltpu.roll(packed, LANES - EDGE * spot - 2, 1)


def folded(packed, width):
    groups = LANES // width
    rows = packed.shape[0] // groups
    lane = lax.broadcasted_iota(jnp.int32, (rows, LANES), 1)
    result = packed[0:rows]
    for group in range(1, groups):
        moved = pltpu.roll(packed[group * rows:(group + 1) * rows], group * width, 1)
        result = jnp.where(lane // width == group, moved, result)
    return result


def unfolded(values, width):
    groups = LANES // width
    return jnp.concatenate(
        [values] + [pltpu.roll(values, LANES - group * width, 1) for group in range(1, groups)], axis=0
    )


class Shifts:
    def __init__(self, nz):
        self.nz = nz
        self.row = row_iota(nz)
        self.lane = lane_iota(nz)

    def z_up(self, value):
        return jnp.where(self.row == self.nz - 1, 0.0, pltpu.roll(value, self.nz - 1, 0))

    def z_down(self, value):
        return jnp.where(self.row == 0, 0.0, pltpu.roll(value, 1, 0))

    def y_up(self, tiles):
        moved = [pltpu.roll(value, LANES - 1, 1) for value in tiles]
        count = len(tiles)
        return [jnp.where(self.lane == LANES - 1, moved[(t + 1) % count], moved[t]) for t in range(count)]

    def y_down(self, tiles):
        moved = [pltpu.roll(value, 1, 1) for value in tiles]
        count = len(tiles)
        return [jnp.where(self.lane == 0, moved[(t - 1) % count], moved[t]) for t in range(count)]


def turn(real_part, imag_part, cosine, sine):
    return real_part * cosine - imag_part * sine, real_part * sine + imag_part * cosine


def inverse_eps(material, levels):
    level = levels[0]
    for index in range(1, len(levels)):
        level = jnp.where(material == index, levels[index], level)
    return 1.0 / level


AHEAD, BACK, EDGES, WAVE, TURNED, LEVELS = 0, 2, 4, 8, 16, 24


def spot_of(run, part, comp):
    return (run * 2 + part) * 6 + comp


class Local:
    def __init__(self, dims, field_ref, edge_ref, small_ref, half_ref, mask_ref):
        self.nz, self.width_x, self.tiles = dims
        self.field_ref, self.edge_ref = field_ref, edge_ref
        self.small_ref, self.half_ref, self.mask_ref = small_ref, half_ref, mask_ref
        self.shifts = Shifts(self.nz)

    def rows(self, x, t):
        return pl.ds(t * self.width_x + x, self.nz, stride=self.tiles * self.width_x)

    def own(self, run, part, comp, x, t):
        return self.field_ref[spot_of(run, part, comp), self.rows(x, t), :]

    def edge(self, x):
        return self.edge_ref[x * self.nz:(x + 1) * self.nz, :]

    def small(self, row):
        return self.small_ref[row:row + 1, :]

    def angle(self, row, run):
        sine = self.small(row + 1)
        return self.small(row), sine if run == 0 else -sine

    def levels(self):
        return [self.small(row) for row in range(LEVELS, self.small_ref.shape[0])]

    def load(self, run, comp, x):
        packed = self.edge(x)
        parts = [[self.own(run, part, comp, x, t) for t in range(self.tiles)] for part in range(2)]
        edges = [unpack_edge(packed, spot_of(run, part, comp)) for part in range(2)]
        edges = turn(edges[0], edges[1], *self.angle(EDGES, run))
        return [parts[part] + [edges[part]] for part in range(2)]

    def half(self, x):
        starts = [(x * self.tiles + t) * self.nz for t in range(self.tiles)]
        own = [self.half_ref[at:at + self.nz, :] for at in starts]
        return own + [COURANT * inverse_eps(unpack_edge(self.edge(x), 24), self.levels())]

    def source(self, run, step, x):
        parts = []
        for part in range(2):
            values = []
            for t in range(self.tiles + 1):
                at = ((run * self.width_x + x) * (self.tiles + 1) + t) * self.nz
                row = (WAVE if t < self.tiles else TURNED) + (run * 2 + part) * 2 + step
                values.append(self.mask_ref[at:at + self.nz, :] * self.small(row))
            parts.append(values)
        return parts


def face_kernel(dims, field_hbm, face_ref, planes_ref, sems):
    nz, width_x, tiles = dims
    copies = [
        pltpu.make_async_copy(field_hbm.at[pl.ds(6 * pair + 1, 2)], planes_ref.at[pair], sems.at[pair])
        for pair in range(4)
    ]
    for copy in copies:
        copy.start()
    for pair in range(4):
        copies[pair].wait()
        for which in range(2):
            values = [planes_ref[pair, which, pl.ds(t * width_x, nz, stride=tiles * width_x), :] for t in range(tiles)]
            store_tiles(face_ref, pair * 2 + which, values, tiles, nz)


def edge_kernel(dims, order_ref, field_ref, material_ref, edge_ref):
    nz, width_x, tiles = dims
    local = Local(dims, field_ref, None, None, None, None)
    lane = lane_iota(nz)
    for x in range(width_x):
        values = []
        for run in range(2):
            for part in range(2):
                for comp in range(6):
                    values.append(
                        jnp.where(
                            lane < LANES // 2,
                            local.own(run, part, comp, x, 0),
                            local.own(run, part, comp, x, tiles - 1),
                        )
                    )
        material = jnp.where(
            lane < LANES // 2, material_ref[local.rows(x, 0), :], material_ref[local.rows(x, tiles - 1), :]
        )
        values.append(material.astype(jnp.float32))
        edge_ref[x * nz:(x + 1) * nz, :] = pack_edges(values, lane)


def prepare_kernel(
    dims, order_ref, material_ref, table_ref, phase_ref, cells_ref, wave_ref, small_ref, half_ref, mask_ref,
):
    nz, width_x, tiles = dims
    row = lax.broadcasted_iota(jnp.int32, (8, LANES), 0)
    angle = jnp.where(row == 0, phase_ref[0], phase_ref[1])
    cosine, sine = jnp.cos(angle), jnp.sin(angle)
    cosine_x, sine_x, cosine_y, sine_y = cosine[0:1], sine[0:1], cosine[1:2], sine[1:2]
    first_x, first_y = lax.axis_index("gx") == 0, lax.axis_index("gy") == 0
    last_x = lax.axis_index("gx") == lax.axis_size("gx") - 1
    last_y = lax.axis_index("gy") == lax.axis_size("gy") - 1
    small_ref[AHEAD:AHEAD + 1, :] = jnp.where(last_x, cosine_x, 1.0)
    small_ref[AHEAD + 1:AHEAD + 2, :] = jnp.where(last_x, sine_x, 0.0)
    small_ref[BACK:BACK + 1, :] = jnp.where(first_x, cosine_x, 1.0)
    small_ref[BACK + 1:BACK + 2, :] = jnp.where(first_x, -sine_x, 0.0)
    upper = lax.broadcasted_iota(jnp.int32, (1, LANES), 1) < LANES // 2
    cosine = jnp.where(upper, jnp.where(last_y, cosine_y, 1.0), jnp.where(first_y, cosine_y, 1.0))
    sine = jnp.where(upper, jnp.where(last_y, sine_y, 0.0), jnp.where(first_y, -sine_y, 0.0))
    small_ref[EDGES:EDGES + 1, :] = cosine
    small_ref[EDGES + 1:EDGES + 2, :] = sine
    small_ref[EDGES + 2:WAVE, :] = jnp.zeros((WAVE - EDGES - 2, LANES), jnp.float32)
    for run in range(2):
        for step in range(2):
            spots = [(run * 2 + part) * 2 + step for part in range(2)]
            amplitude = [wave_ref[0, run, part, step] for part in range(2)]
            turned = turn(amplitude[0], amplitude[1], cosine, sine if run == 0 else -sine)
            for part in range(2):
                row = WAVE + spots[part]
                small_ref[row:row + 1, :] = jnp.full((1, LANES), amplitude[part], jnp.float32)
                row = TURNED + spots[part]
                small_ref[row:row + 1, :] = turned[part]
    for index in range(table_ref.shape[0]):
        small_ref[LEVELS + index:LEVELS + index + 1, :] = jnp.full((1, LANES), table_ref[index], jnp.float32)
    levels = [table_ref[index] for index in range(table_ref.shape[0])]
    total_x = width_x * lax.axis_size("gx")
    width_y = tiles * LANES
    total_y = width_y * lax.axis_size("gy")
    begin_y = lax.axis_index("gy") * width_y
    z, lane = row_iota(nz), lane_iota(nz)
    for x in range(width_x):
        plane = z * total_x + lax.axis_index("gx") * width_x + x
        for t in range(tiles + 1):
            if t < tiles:
                column = begin_y + t * LANES + lane
                material = material_ref[pl.ds(t * width_x + x, nz, stride=tiles * width_x), :]
                at = (x * tiles + t) * nz
                half_ref[at:at + nz, :] = COURANT * inverse_eps(material, levels)
            else:
                column = begin_y + jnp.where(lane < LANES // 2, lane + width_y, lane - LANES)
                column = jnp.where(column < 0, column + total_y, column)
                column = jnp.where(column >= total_y, column - total_y, column)
            index = plane * total_y + column
            for run in range(2):
                at = ((run * width_x + x) * (tiles + 1) + t) * nz
                mask_ref[at:at + nz, :] = jnp.where(index == cells_ref[0, run], 1.0, 0.0)


def merged_edges(below_ref, above_ref, edge_ref):
    if above_ref is None:
        return below_ref
    lane = lax.broadcasted_iota(jnp.int32, below_ref.shape, 1)
    edge_ref[...] = jnp.where(lane % EDGE < 2, below_ref[...], above_ref[...])
    return edge_ref


def small_steps(local, ex, ey, ez, hx, hy, hz, ey_x, ez_x):
    shifts = local.shifts
    every = range(len(ex))
    ez_y, ex_y = shifts.y_up(ez), shifts.y_up(ex)
    new_x = None
    if hx is not None:
        new_x = [hx[t] - COURANT * (ez_y[t] - ez[t] - (shifts.z_up(ey[t]) - ey[t])) for t in every]
    diff_z = [-ez[t] if ez_x is None else ez_x[t] - ez[t] for t in every]
    diff_y = [-ey[t] if ey_x is None else ey_x[t] - ey[t] for t in every]
    new_y = [hy[t] - COURANT * (shifts.z_up(ex[t]) - ex[t] - diff_z[t]) for t in every]
    new_z = [hz[t] - COURANT * (diff_y[t] - (ex_y[t] - ex[t])) for t in every]
    return new_x, new_y, new_z


def grown(local, ex, ey, ez, hx, hy, hz, hy_x, hz_x, half, source, count):
    shifts = local.shifts
    hz_y, hx_y = shifts.y_down(hz), shifts.y_down(hx)
    new_x, new_y, new_z = [], [], []
    for t in range(count):
        diff_y = hz[t] if hz_x is None else hz[t] - hz_x[t]
        diff_z = hy[t] if hy_x is None else hy[t] - hy_x[t]
        if ex is not None:
            new_x.append(ex[t] + half[t] * (hz[t] - hz_y[t] - (hy[t] - shifts.z_down(hy[t]))))
        new_y.append(ey[t] + half[t] * (hx[t] - shifts.z_down(hx[t]) - diff_y))
        new_z.append(ez[t] + half[t] * (diff_z - (hx[t] - hx_y[t])) + source[t])
    return new_x, new_y, new_z


def started(dims, two, field_ref, below_ref, above_ref, small_ref, half_ref, mask_ref, edge_ref):
    edges = merged_edges(below_ref, None if two else above_ref, edge_ref)
    return Local(dims, field_ref, edges, small_ref, half_ref, mask_ref)


def store_tiles(ref, unit, values, tiles, nz):
    for t in range(tiles):
        at = (unit * tiles + t) * nz
        ref[at:at + nz, :] = values[t]


def lower_kernel(dims, two, *refs):
    nz, _, tiles = dims
    *given, material_ref, down_ref, edge_ref = refs
    local = started(dims, two, *given, edge_ref)
    local.material = [material_ref[local.rows(0, t), :].astype(jnp.float32) for t in range(tiles)]
    half = local.half(0)
    edges = [None] * 16
    for run in range(2):
        low = [local.load(run, comp, 0) for comp in range(6)]
        nearer = [local.load(run, comp, 1) for comp in (1, 2)]
        source = local.source(run, 0, 0)
        for part in range(2):
            ex, ey, ez, hx, hy, hz = [low[comp][part] for comp in range(6)]
            hx, hy, hz = small_steps(local, ex, ey, ez, hx, hy, hz, nearer[0][part], nearer[1][part])
            _, new_y, new_z = grown(local, None, ey, ez, hx, hy, hz, None, None, half, source[part], tiles + 1)
            for which, value, initial in ((0, new_y, ey), (1, new_z, ez)):
                unit = (run * 2 + part) * 2 + which
                store_tiles(down_ref, unit, value, tiles, nz)
                edges[unit] = initial[tiles]
                edges[8 + unit] = value[tiles]
    store_tiles(down_ref, 8, local.material, tiles, nz)
    packed = pack_edges(edges, local.shifts.lane)
    column = pltpu.roll(unpack_edge(local.edge(0), 24), LANES - MATERIAL_MOVE, 1)
    packed = jnp.where(local.shifts.lane == EDGE * 8, column, packed)
    down_ref[9 * tiles * nz:, :] = folded(packed, 64)


def upper_kernel(dims, two, *refs):
    nz, width_x, tiles = dims
    *given, _, up_ref, edge_ref = refs
    local = started(dims, two, *given, edge_ref)
    edges = []
    for run in range(2):
        high = [local.load(run, comp, width_x - 1) for comp in (0, 1, 2, 4, 5)]
        for part in range(2):
            ex, ey, ez, hy, hz = [values[part] for values in high]
            _, hy, hz = small_steps(local, ex, ey, ez, None, hy, hz, None, None)
            for which, value in ((0, hy), (1, hz)):
                store_tiles(up_ref, (run * 2 + part) * 2 + which, value, tiles, nz)
                edges.append(value[tiles])
    up_ref[8 * tiles * nz:, :] = folded(pack_edges(edges, local.shifts.lane), 32)


def halo(local, ref, edge, first_spot, run, which, row):
    nz, tiles = local.nz, local.tiles
    units = [(run * 2 + part) * 2 + which for part in range(2)]
    values = [
        [ref[(unit * tiles + t) * nz:(unit * tiles + t + 1) * nz, :] for t in range(tiles)]
        + [unpack_edge(edge, first_spot + unit)]
        for unit in units
    ]
    turned = [turn(values[0][t], values[1][t], *local.angle(row, run)) for t in range(tiles + 1)]
    return [[value[part] for value in turned] for part in range(2)]


def half_above(local, down_ref, edge):
    nz, tiles = local.nz, local.tiles
    own = [down_ref[(8 * tiles + t) * nz:(8 * tiles + t + 1) * nz, :] for t in range(tiles)]
    levels = local.levels()
    return [COURANT * inverse_eps(value, levels) for value in own + [pltpu.roll(edge, MATERIAL_MOVE, 1)]]


def wide(ref, unit, nz, count):
    return [ref[(unit * count + t) * nz:(unit * count + t + 1) * nz, :] for t in range(count)]


def early_kernel(dims, two, *refs):
    nz, width_x, tiles = dims
    *given, _, early_ref, edge_ref = refs
    local = started(dims, two, *given, edge_ref)
    every = range(tiles + 1)
    half = [local.half(x) for x in range(width_x - 1)]
    for run in range(2):
        sources = [local.source(run, 0, x) for x in range(width_x - 1)]
        fields = [[local.load(run, comp, x) for x in range(width_x - 1)] for comp in range(6)]
        highest = [local.load(run, comp, width_x - 1) for comp in (1, 2)]
        for part in range(2):
            pair = run * 2 + part
            under_y = [COURANT * value for value in fields[2][0][part]]
            under_z = [-COURANT * value for value in fields[1][0][part]]
            for x in range(width_x - 1):
                ex, ey, ez, hx, hy, hz = [fields[comp][x][part] for comp in range(6)]
                if x < width_x - 2:
                    ey_x, ez_x = fields[1][x + 1][part], fields[2][x + 1][part]
                else:
                    ey_x, ez_x = highest[0][part], highest[1][part]
                hx, hy, hz = small_steps(local, ex, ey, ez, hx, hy, hz, ey_x, ez_x)
                new = grown(local, ex, ey, ez, hx, hy, hz, under_y, under_z, half[x], sources[x][part], tiles + 1)
                for comp, value in enumerate((*new, hx, hy, hz)):
                    store_tiles(early_ref, (pair * (width_x - 1) + x) * 6 + comp, value, tiles + 1, nz)
                under_y, under_z = hy, hz


def share_kernel(dims, two, *refs):
    nz, width_x, tiles = dims
    *given, face_ref, down_ref, early_ref, share_ref, high_ref, edge_ref = refs
    local = started(dims, two, *given, edge_ref)
    edge = unfolded(down_ref[9 * tiles * nz:, :], 64)
    half = local.half(width_x - 1)
    above = half_above(local, down_ref, edge)
    kept_e, kept_h = {}, {}
    every = range(tiles + 1)
    for run in range(2):
        high = [local.load(run, comp, width_x - 1) for comp in range(6)]
        source = local.source(run, 0, width_x - 1)
        early = [halo(local, face_ref, edge, 0, run, which, AHEAD) for which in range(2)]
        later = [halo(local, down_ref, edge, 8, run, which, AHEAD) for which in range(2)]
        for part in range(2):
            pair = run * 2 + part
            ex, ey, ez, hx, hy, hz = [high[comp][part] for comp in range(6)]
            low = (pair * (width_x - 1) + width_x - 2) * 6
            low_hy, low_hz = [wide(early_ref, low + comp, nz, tiles + 1) for comp in (4, 5)]
            hx, hy, hz = small_steps(local, ex, ey, ez, hx, hy, hz, early[0][part], early[1][part])
            ex, ey, ez = grown(local, ex, ey, ez, hx, hy, hz, low_hy, low_hz, half, source[part], tiles + 1)
            above_y = [later[0][part][t] + above[t] * hz[t] for t in every]
            above_z = [later[1][part][t] - above[t] * hy[t] for t in every]
            _, hy, hz = small_steps(local, ex, ey, ez, None, hy, hz, above_y, above_z)
            kept_e[run, part] = (above_y, above_z)
            kept_h[run, part] = (hy, hz)
            for comp, value in enumerate((ex, ey, ez, hx, hy, hz)):
                store_tiles(high_ref, pair * 6 + comp, value, tiles + 1, nz)
    for t in range(tiles):
        total = 0.0
        for run in range(2):
            for which, sign in ((0, 1.0), (1, -1.0)):
                term = (
                    kept_e[run, 0][which][t] * kept_h[1 - run, 0][1 - which][t]
                    - kept_e[run, 1][which][t] * kept_h[1 - run, 1][1 - which][t]
                )
                total = total + sign * term
        share_ref[t * nz:(t + 1) * nz, :] = above[t] * total


def product(now, later, t):
    return now[0, 0][t] * later[1, 0][t] - now[0, 1][t] * later[1, 1][t]


def both(one, two, t):
    return product(one, two, t) + product(two, one, t)


def interior_kernel(dims, two, *refs):
    nz, width_x, tiles = dims
    *given, early_ref, high_ref, _, kept_ref, cross_ref, edge_ref = refs
    local = started(dims, two, *given, edge_ref)
    shifts = local.shifts
    every, own, layers = range(tiles + 1), range(tiles), range(width_x)
    half = [local.half(x) for x in layers]
    kept_one, kept_two = {}, {}
    for run in range(2):
        sources = [local.source(run, 1, x) for x in layers]
        for part in range(2):
            pair = run * 2 + part
            fields = []
            for x in range(width_x - 1):
                first = (pair * (width_x - 1) + x) * 6
                fields.append([wide(early_ref, first + comp, nz, tiles + 1) for comp in range(6)])
            fields.append([wide(high_ref, pair * 6 + comp, nz, tiles + 1) for comp in range(6)])
            hy_x, hz_x = None, None
            for x in layers:
                ex, ey, ez, hx, hy, hz = fields[x]
                if x < width_x - 1:
                    hx, hy, hz = small_steps(local, ex, ey, ez, hx, hy, hz, fields[x + 1][1], fields[x + 1][2])
                else:
                    ez_y = shifts.y_up(ez)
                    hx = [hx[t] - COURANT * (ez_y[t] - ez[t] - (shifts.z_up(ey[t]) - ey[t])) for t in every]
                new = grown(local, ex, ey, ez, hx, hy, hz, hy_x, hz_x, half[x], sources[x][part], tiles)
                hy_x, hz_x = hy, hz
                for comp in range(3):
                    kept_one.setdefault((comp, x), {})[run, part] = fields[x][comp]
                    kept_two.setdefault((comp, x), {})[run, part] = new[comp]
    for pair in range(4):
        where = (pair // 2, pair % 2)
        for comp in range(3):
            store_tiles(kept_ref, pair * 8 + comp, kept_one[comp, 0][where], tiles, nz)
            store_tiles(kept_ref, pair * 8 + 3 + comp, kept_two[comp, 0][where], tiles, nz)
        for comp in (1, 2):
            store_tiles(kept_ref, pair * 8 + 5 + comp, kept_one[comp, 1][where], tiles, nz)
    store_tiles(kept_ref, 32, half[0], tiles, nz)
    at = 33 * tiles * nz
    kept_ref[at:at + nz, :] = half[0][tiles]
    for x in range(1, width_x):
        for t in own:
            total = 0.0
            for comp in range(3):
                total = total + both(kept_one[comp, x], kept_two[comp, x], t)
            cross_ref[local.rows(x, t), :] = -half[x][t] * total
    for t in own:
        cross_ref[local.rows(0, t), :] = half[0][t]


def final_kernel(dims, small_ref, half_ref, kept_ref, inner_ref, up_ref, *cross_refs):
    nz, width_x, tiles = dims
    local = Local(dims, None, None, small_ref, half_ref, None)
    shifts = local.shifts
    every, own = range(tiles + 1), range(tiles)

    def tile(ref, unit, t):
        return ref[(unit * tiles + t) * nz:(unit * tiles + t + 1) * nz, :]

    half = [tile(kept_ref, 32, t) for t in every]
    next_half = [tile(half_ref, 1, t) for t in own]
    edge = unfolded(up_ref[8 * tiles * nz:, :], 32)
    one, two, next_one, next_add = [[{} for _ in range(3)] for _ in range(4)]
    for run in range(2):
        under = [halo(local, up_ref, edge, 0, run, which, BACK) for which in range(2)]
        for part in range(2):
            pair = run * 2 + part
            add_y = [half[t] * under[1][part][t] for t in every]
            add_z = [-half[t] * under[0][part][t] for t in every]
            add_z_y = shifts.y_up(add_z)
            hx = [-COURANT * (add_z_y[t] - add_z[t] - (shifts.z_up(add_y[t]) - add_y[t])) for t in every]
            hy = [-COURANT * add_z[t] for t in every]
            hz = [COURANT * add_y[t] for t in every]
            hz_y, hx_y = shifts.y_down(hz), shifts.y_down(hx)
            more = [
                [half[t] * (hz[t] - hz_y[t] - (hy[t] - shifts.z_down(hy[t]))) for t in own],
                [add_y[t] + half[t] * (hx[t] - shifts.z_down(hx[t]) - hz[t]) for t in own],
                [add_z[t] + half[t] * (hy[t] - (hx[t] - hx_y[t])) for t in own],
            ]
            first = [None, add_y, add_z]
            for comp in range(3):
                value = [tile(kept_ref, pair * 8 + comp, t) for t in own]
                one[comp][run, part] = value if comp == 0 else [value[t] + first[comp][t] for t in own]
                two[comp][run, part] = [tile(kept_ref, pair * 8 + 3 + comp, t) + more[comp][t] for t in own]
            for comp, value in ((1, hz), (2, [-hy[t] for t in own])):
                next_one[comp][run, part] = [tile(kept_ref, pair * 8 + 5 + comp, t) for t in own]
                next_add[comp][run, part] = [next_half[t] * value[t] for t in own]
    for t in own:
        for x in range(width_x):
            if x == 0:
                total = 0.0
                for comp in range(3):
                    total = total + both(one[comp], two[comp], t)
                total = -half[t] * total
            else:
                total = inner_ref[local.rows(x, t), :]
                if x == 1:
                    total = total - next_half[t] * (
                        both(next_one[1], next_add[1], t) + both(next_one[2], next_add[2], t)
                    )
            cross_refs[x][t * nz:(t + 1) * nz, :] = total


def sum_kernel(dims, half_ref, own_share_ref, other_share_ref, *refs):
    nz, width_x, tiles = dims
    *parts, out_ref = refs
    for x in range(width_x):
        for t in range(tiles):
            span = slice(t * nz, (t + 1) * nz)
            total = parts[x][span, :] + parts[width_x + x][span, :]
            if x == 0:
                total = total - half_ref[span, :] * (own_share_ref[span, :] + other_share_ref[span, :])
            out_ref[pl.ds(t * width_x + x, nz, stride=tiles * width_x), :] = total


VMEM = pl.BlockSpec(memory_space=pltpu.VMEM)
SMEM = pl.BlockSpec(memory_space=pltpu.SMEM)


HBM = pl.BlockSpec(memory_space=pltpu.HBM)
MIB = 1024 * 1024


def call(kernel, name, in_specs, rows, cost, scratch=(), limit=48 * MIB):
    shapes = [jax.ShapeDtypeStruct((count, LANES), jnp.float32) for count in rows]
    return pl.pallas_call(
        kernel,
        name=name,
        out_shape=shapes,
        in_specs=in_specs,
        out_specs=[VMEM] * len(shapes),
        scratch_shapes=list(scratch),
        compiler_params=pltpu.CompilerParams(vmem_limit_bytes=limit),
        cost_estimate=pl.CostEstimate(flops=0, bytes_accessed=cost, transcendentals=0),
    )


def moved(value, axis, steps):
    count = lax.axis_size(axis)
    return lax.ppermute(value, axis, [(source, (source + steps) % count) for source in range(count)])


def local(field_state, material_map, eps_table, bloch_phase, source_cells, source_wave):
    nz, width_x, width_y = material_map.shape
    tiles = width_y // LANES
    dims = (nz, width_x, tiles)
    rows = nz * tiles * width_x
    fields = field_state.reshape(24, nz, width_x, tiles, LANES).transpose(0, 1, 3, 2, 4).reshape(24, rows, LANES)
    material = material_map.reshape(nz, width_x, tiles, LANES).transpose(0, 2, 1, 3).reshape(rows, LANES)
    unit = nz * tiles
    two = lax.axis_size("gy") == 2
    levels = eps_table.shape[0]

    (face,) = call(
        functools.partial(face_kernel, dims), "faces", [HBM], [8 * unit], 100_000,
        (pltpu.VMEM((4, 2, rows, LANES), jnp.float32), pltpu.SemaphoreType.DMA((4,))),
        53 * MIB,
    )(fields)
    (edge,) = call(functools.partial(edge_kernel, dims), "edges", [VMEM] * 3, [width_x * nz], 80_000_000)(
        face, fields, material
    )
    small, half, mask = call(
        functools.partial(prepare_kernel, dims), "prepare", [VMEM] * 2 + [SMEM] * 4,
        [LEVELS + levels, rows, 2 * width_x * (tiles + 1) * nz], 20_000_000,
    )(edge, material, eps_table, bloch_phase, source_cells, source_wave)
    face = moved(face, "gx", -1)
    below = moved(edge, "gy", 1)
    above = below if two else moved(edge, "gy", -1)
    given = (fields, below, above, small, half, mask)
    specs = [VMEM] * len(given)
    scratch = (pltpu.VMEM((width_x * nz, LANES), jnp.float32),)

    def stage(kernel, name, cost, rows, *more):
        return call(
            functools.partial(kernel, dims, two), name, specs + [VMEM] * len(more), rows, cost, scratch
        )(*given, *more)

    down = moved(stage(lower_kernel, "lower", 20_000_000, [9 * unit + nz // 2], material)[0], "gx", -1)
    up = moved(stage(upper_kernel, "upper", 20_000_000, [8 * unit + nz // 4], face)[0], "gx", 1)
    wide_unit = (tiles + 1) * nz
    (early,) = stage(early_kernel, "early", 20_000_000, [24 * (width_x - 1) * wide_unit], face)
    share, high = stage(share_kernel, "share", 20_000_000, [unit, 24 * wide_unit], face, down, early)
    count_x, count_src = lax.axis_size("gx"), lax.axis_size("src")
    own_share = moved(share, "gx", 1)
    other_share = lax.ppermute(
        share, ("gx", "src"),
        [
            (x * count_src + s, (x + 1) % count_x * count_src + (s + 1) % count_src)
            for x in range(count_x)
            for s in range(count_src)
        ],
    )
    kept, inner = stage(interior_kernel, "interior", 40_000_000, [33 * unit + nz, rows], early, high, share)
    cross = call(
        functools.partial(final_kernel, dims), "final", [VMEM] * 5, [unit] * width_x, 1_000_000
    )(small, half, kept, inner, up)
    other = [moved(value, "src", 1) for value in cross]
    (out,) = call(
        functools.partial(sum_kernel, dims), "gradient", [VMEM] * (3 + 2 * len(other)), [rows], 10_000
    )(half, own_share, other_share, *cross, *other)
    return out.reshape(nz, tiles, width_x, LANES).transpose(0, 2, 1, 3).reshape(nz, width_x, width_y)


def solution(mesh):
    return jax.shard_map(
        local,
        mesh=mesh,
        in_specs=(
            P(("design", "src"), None, None, None, None, "gx", "gy"),
            P("design", "gx", "gy"),
            P(),
            P("design"),
            P(("design", "src"), None),
            P(("design", "src"), None, None, None),
        ),
        out_specs=P("design", "gx", "gy"),
        check_vma=False,
    )
```
